128 devices in a mesh: batch: 4 (over z), seq: 32 (over y, x, core).
Axes of the slice: x: 4, y: 4, z: 4, core: 2. Of those that a mesh axis runs over, the one named last changes fastest.
Arguments:
- packed: bfloat16 [131072, 768], P(('batch', 'seq')), may hold values from -5 to 5
- block_dest: int32 [4096], P(('batch', 'seq')), may hold values from 0 to 1023, as said below
- doc_len: int32 [20], P('batch'), may hold values from 6400 to 8192, as said below
- w_qkv: bfloat16 [768, 2304], replicated
- b_qkv: float32 [2304], replicated, may hold values from -3 to 3
- w_out: bfloat16 [768, 768], replicated, may hold values from -0.21875 to 0.21875
- b_out: float32 [768], replicated, may hold values from -3 to 3
- norm1_gain: float32 [768], replicated, may hold values from 0.1 to 1.9
- norm1_shift: float32 [768], replicated, may hold values from -2 to 2
- w_glu: bfloat16 [768, 6144], replicated, may hold values from -0.21875 to 0.21875
- w_down: bfloat16 [3072, 768], replicated, may hold values from -0.109375 to 0.109375
- b_down: float32 [768], replicated, may hold values from -3 to 3
- norm2_gain: float32 [768], replicated, may hold values from 0.1 to 1.9
- norm2_shift: float32 [768], replicated, may hold values from -2 to 2
- centroids: bfloat16 [256, 768], replicated, may hold values from -3 to 3
- tile_list: int32 [512], P(('batch', 'seq')), may hold values from 0 to 255, as said below
Outputs:
- encoded: bfloat16 [131072, 768], P(('batch', 'seq'))
- stored: bfloat16 [4, 32, 1024, 768], P('batch', 'seq')
The draws below stay inside these ranges and needn't reach their ends.
Inputs may be any that keep to these rules, and one draw needn't show every extreme that they name: `block_dest`: within a group, the entries of its 32 devices form a permutation of the group's block positions; position q is block q % 32 of sequence shard q // 32. At most 2 blocks of one device go to one shard. `doc_len`: valid tokens counted from the document's start in the stream. `tile_list`: list // 64 is the batch index that owns the list; at most 2 tiles of one device share an owner.
All inputs are finite; a program needn't handle non-finite values.
Results may differ from the reference program's by a relative error of at most 0.011.
Values may be sent and summed in bfloat16 or wider, within the bound.
No kernel may reach another device: no remote copies, remote signals or barrier semaphores. Data moves between devices by JAX's collectives and lax.ppermute only.
A program may use at most 192 MiB of HBM per device.

```python
import math
import jax
import jax.numpy as jnp
import numpy as np
from jax import lax

D = 768
H = 12
FF = 3072
S_DEV = 1024
DOC_LEN = 8192
BAND = 256
STRETCH = 2
TROWS = 128
LPO = 64
LEAD = 512
TOKENS = 131072
DOCS_GRP = 5
DOCS = 20
TILES_DEV = 4
CAPT = 2
NLIST = 256
N_BATCH = 4
N_SEQ = 32


def shuffles(key, count, length):
    return jax.vmap(lambda single: jax.random.permutation(single, length))(jax.random.split(key, count))


def draw_block_dest(key, part):
    key = jax.random.fold_in(key, 11)
    keys = jax.random.split(key, 4)
    slots = jnp.arange(N_SEQ, dtype=jnp.int32)
    doubled = jax.random.randint(keys[0], (N_BATCH, 1), 1, N_SEQ // 2 + 1)
    spread = shuffles(keys[1], N_BATCH, N_SEQ)
    grouping = jnp.where(slots[None, :] < 2 * doubled, slots[None, :] // 2, slots[None, :] - doubled)
    offset = jnp.take_along_axis(spread, grouping, axis=1)
    target = (slots[None, :, None] + offset[:, None, :]) % N_SEQ
    inner = shuffles(keys[2], N_BATCH * N_SEQ, N_SEQ).reshape(N_BATCH, N_SEQ, N_SEQ)
    within = jax.vmap(lambda table, rows_at: table[rows_at, slots[None, :]])(inner, target)
    value = target * N_SEQ + within
    order = shuffles(keys[3], N_BATCH * N_SEQ, N_SEQ).reshape(N_BATCH, N_SEQ, N_SEQ)

    def place(values_row, order_row):
        return jnp.zeros_like(values_row).at[order_row].set(values_row)
    result = jax.vmap(jax.vmap(place))(value, order)
    return result.reshape(-1).astype(jnp.int32)


def draw_doc_len(key, part):
    key = jax.random.fold_in(key, 23)
    shortest = 3 * DOC_LEN // 4 + BAND
    lens = jax.random.randint(key, (DOCS,), shortest, DOC_LEN + 1)
    return lens.at[0].set(DOC_LEN).at[1].set(shortest).astype(jnp.int32)


def draw_tile_list(key, part):
    key = jax.random.fold_in(key, 37)
    keys = jax.random.split(key, 7)
    devices_all = N_BATCH * N_SEQ
    first = jax.random.randint(keys[0], (devices_all,), 0, N_BATCH)
    second = jax.random.randint(keys[1], (devices_all,), 0, N_BATCH)
    main = jnp.minimum(first, second)
    column = jax.random.randint(keys[2], (), 2, N_SEQ)
    chosen = jax.random.randint(keys[3], (), 0, N_BATCH)
    indices = jnp.arange(devices_all, dtype=jnp.int32)
    main = jnp.where(indices % N_SEQ == column, chosen, main)
    main = main.at[0].set(N_BATCH - 1).at[1].set(0)
    steps = jax.random.randint(keys[4], (devices_all, TILES_DEV - CAPT), 1, N_BATCH)
    others = (main[:, None] + steps) % N_BATCH
    owners = jnp.concatenate([jnp.broadcast_to(main[:, None], (devices_all, CAPT)), others], axis=1)
    offsets = jax.random.randint(keys[5], (devices_all, TILES_DEV), 0, LPO)
    offsets = offsets.at[0, 0].set(LPO - 1).at[1, 0].set(0)
    lists = owners * LPO + offsets
    order = shuffles(keys[6], devices_all, TILES_DEV)
    return jnp.take_along_axis(lists, order, axis=1).reshape(-1).astype(jnp.int32)


def draw_w_qkv(key, part):
    key = jax.random.fold_in(key, 41)
    base = jnp.clip(jax.random.normal(key, (D, 3 * D), jnp.float32), -4.0, 4.0) * D ** (-0.5)
    return base.astype(jnp.bfloat16)


def steps_of(key, extent, cuts, least, largest):
    level, own = 1.0, jax.random.fold_in(key, 6)
    for position, shards_of in cuts:
        draws = jnp.exp(jax.random.uniform(jax.random.fold_in(own, position), (shards_of,), jnp.float32, least / len(cuts), largest / len(cuts)))
        level = level * jnp.repeat(draws, extent[position] // shards_of).reshape([-1 if axis == position else 1 for axis in range(len(extent))])
    return level


def noise(key, dims, scale, reach, shards=(), kind=jnp.bfloat16):
    level = steps_of(key, dims, shards, -0.22, 0.18) if shards else 1.0
    drawn = jax.random.normal(key, dims, jnp.float32) * scale * level
    return jnp.minimum(jnp.maximum(drawn, -reach), reach).astype(kind)


def setup_inputs(seed: int = 0) -> dict:
    key_of = jax.random.split(jax.random.key(seed), 17)
    packed = noise(key_of[0], (TOKENS, D), 1.0, 5.0, ((0, 128),))
    block_dest = draw_block_dest(jax.random.fold_in(key_of[16], 71), 0)
    doc_len = draw_doc_len(jax.random.fold_in(key_of[16], 71), 0)
    w_qkv = draw_w_qkv(jax.random.fold_in(key_of[16], 71), 0)
    b_qkv = noise(key_of[4], (3 * D,), 0.5, 3.0, (), jnp.float32)
    w_out = noise(key_of[5], (D, D), D ** -0.5, 0.21875)
    b_out = noise(key_of[6], (D,), 0.5, 3.0, (), jnp.float32)
    norm1_gain = jnp.clip(1.0 + 0.18 * jax.random.normal(key_of[7], (D,), jnp.float32), 0.1, 1.9)
    norm1_shift = noise(key_of[8], (D,), 0.3, 2.0, (), jnp.float32)
    w_glu = noise(key_of[9], (D, 2 * FF), D ** -0.5, 0.21875)
    w_down = noise(key_of[10], (FF, D), FF ** -0.5, 0.109375)
    b_down = noise(key_of[11], (D,), 0.5, 3.0, (), jnp.float32)
    norm2_gain = jnp.clip(1.0 + 0.18 * jax.random.normal(key_of[12], (D,), jnp.float32), 0.1, 1.9)
    norm2_shift = noise(key_of[13], (D,), 0.3, 2.0, (), jnp.float32)
    centroids = noise(key_of[14], (NLIST, D), 0.5, 3.0)
    tile_list = draw_tile_list(jax.random.fold_in(key_of[16], 71), 0)
    return dict(packed=packed, block_dest=block_dest, doc_len=doc_len, w_qkv=w_qkv, b_qkv=b_qkv, w_out=w_out, b_out=b_out, norm1_gain=norm1_gain, norm1_shift=norm1_shift, w_glu=w_glu, w_down=w_down, b_down=b_down, norm2_gain=norm2_gain, norm2_shift=norm2_shift, centroids=centroids, tile_list=tile_list)


norm_eps = 1e-06
masked_score = -1e+30

def head_slopes(heads):
    base = 2 ** int(np.floor(np.log2(heads)))
    first = [2.0 ** (-8.0 * (i + 1) / base) for i in range(base)]
    extra = [2.0 ** (-4.0 * (i + 1) / base) for i in range(2 * (heads - base))][0::2]
    return jnp.asarray(first + extra, jnp.float32)

def layer_norm(values, gain, shift):
    centre = lax.optimization_barrier(jnp.mean(values, axis=-1, keepdims=True))
    spread = lax.optimization_barrier(jnp.mean(jnp.square(values - centre), axis=-1, keepdims=True))
    return (values - centre) * lax.rsqrt(spread + norm_eps) * gain + shift

def attend(queries, keys, values, query_pos, key_pos, key_live, slopes):
    heads = slopes.shape[0]
    count = queries.shape[0]
    width = queries.shape[1]
    size = width // heads
    query_heads = queries.reshape(count, heads, size).astype(jnp.float32)
    key_heads = keys.reshape(keys.shape[0], heads, size).astype(jnp.float32)
    value_heads = values.reshape(values.shape[0], heads, size).astype(jnp.float32)
    scores = jnp.einsum('qhd,khd->hqk', query_heads, key_heads) * (1.0 / math.sqrt(size))
    distance = jnp.abs(query_pos[:, None] - key_pos[None, :])
    scores = scores - slopes[:, None, None] * distance.astype(jnp.float32)[None]
    same_doc = query_pos[:, None] // DOC_LEN == key_pos[None, :] // DOC_LEN
    allowed = (distance <= BAND) & same_doc & (key_live[None, :] | (distance == 0))
    scores = jnp.where(allowed[None], scores, masked_score)
    top = lax.optimization_barrier(jnp.max(scores, axis=-1, keepdims=True))
    weights = jnp.exp(scores - top)
    probs = (weights / lax.optimization_barrier(jnp.sum(weights, axis=-1, keepdims=True))).astype(jnp.bfloat16)
    mixed = jnp.einsum('hqk,khd->qhd', probs.astype(jnp.float32), value_heads)
    return mixed.astype(jnp.bfloat16).reshape(count, width)

def finish(attended, inputs, w_out, b_out, norm1_gain, norm1_shift, w_glu, w_down, b_down, norm2_gain, norm2_shift):
    mixed = jnp.dot(attended, w_out, preferred_element_type=jnp.float32) + b_out + inputs.astype(jnp.float32)
    first = layer_norm(mixed, norm1_gain, norm1_shift).astype(jnp.bfloat16)
    both = jnp.dot(first, w_glu, preferred_element_type=jnp.float32)
    hidden = w_down.shape[0]
    active = (jax.nn.gelu(both[:, :hidden], approximate=False) * both[:, hidden:]).astype(jnp.bfloat16)
    second = jnp.dot(active, w_down, preferred_element_type=jnp.float32) + b_down + first.astype(jnp.float32)
    return layer_norm(second, norm2_gain, norm2_shift).astype(jnp.bfloat16)

def reference(packed, block_dest, doc_len, w_qkv, b_qkv, w_out, b_out, norm1_gain, norm1_shift, w_glu, w_down, b_down, norm2_gain, norm2_shift, centroids, tile_list):
    span = N_SEQ * S_DEV
    block = S_DEV // N_SEQ
    number = N_SEQ * N_SEQ
    slopes = head_slopes(H)
    pieces = packed.reshape(N_BATCH, number, block, D)
    targets = block_dest.reshape(N_BATCH, number)

    def unpack(group_pieces, group_targets):
        return jnp.zeros_like(group_pieces).at[group_targets].set(group_pieces)
    inputs = jax.vmap(unpack)(pieces, targets).reshape(N_BATCH, span, D)
    lengths = doc_len.reshape(N_BATCH, DOCS_GRP)
    stride = min(512, S_DEV)

    def encode(group):
        source, lens = group
        projected = (jnp.dot(source, w_qkv, preferred_element_type=jnp.float32) + b_qkv).astype(jnp.bfloat16)
        padding = jnp.zeros((BAND, 2 * D), jnp.bfloat16)
        sides = jnp.concatenate([padding, projected[:, D:], padding], axis=0)
        key_pos = jnp.arange(span + 2 * BAND, dtype=jnp.int32) - BAND
        stream_pos = key_pos + LEAD
        key_doc = jnp.clip(stream_pos // DOC_LEN, 0, DOCS_GRP - 1)
        key_live = (key_pos >= 0) & (key_pos < span) & (stream_pos % DOC_LEN < lens[key_doc])

        def one_block(index):
            start = index * stride
            queries = lax.dynamic_slice_in_dim(projected[:, :D], start, stride, 0)
            near = lax.dynamic_slice_in_dim(sides, start, stride + 2 * BAND, 0)
            live = lax.dynamic_slice_in_dim(key_live, start, stride + 2 * BAND, 0)
            near_pos = lax.dynamic_slice_in_dim(stream_pos, start, stride + 2 * BAND, 0)
            query_pos = start + LEAD + jnp.arange(stride, dtype=jnp.int32)
            attended = attend(queries, near[:, :D], near[:, D:], query_pos, near_pos, live, slopes)
            rows_in = lax.dynamic_slice_in_dim(source, start, stride, 0)
            return finish(attended, rows_in, w_out, b_out, norm1_gain, norm1_shift, w_glu, w_down, b_down, norm2_gain, norm2_shift)
        return lax.map(one_block, jnp.arange(span // stride, dtype=jnp.int32)).reshape(span, D)
    encoded = lax.map(encode, (inputs, lengths))
    token_pos = jnp.arange(span, dtype=jnp.int32) + LEAD
    row_len = lengths[:, token_pos // DOC_LEN]
    live_rows = ((token_pos % DOC_LEN)[None, :] < row_len).astype(jnp.float32)
    grouped = encoded.astype(jnp.float32).reshape(N_BATCH, span // STRETCH, STRETCH, D)
    weights = live_rows.reshape(N_BATCH, span // STRETCH, STRETCH, 1)
    pooled = lax.optimization_barrier(jnp.sum(grouped * weights, axis=2)) / jnp.maximum(lax.optimization_barrier(jnp.sum(weights, axis=2)), 1.0)
    tiles = pooled.reshape(N_BATCH, N_SEQ, TILES_DEV, TROWS, D)
    lists = tile_list.reshape(N_BATCH, N_SEQ, TILES_DEV)
    residual = (tiles - centroids.astype(jnp.float32)[lists][:, :, :, None, :]).astype(jnp.bfloat16)
    owners = lists // LPO
    order = jnp.arange(TILES_DEV, dtype=jnp.int32)
    earlier = (owners[..., :, None] == owners[..., None, :]) & (order[None, :] < order[:, None])
    rank = lax.optimization_barrier(jnp.sum(earlier.astype(jnp.int32), axis=-1))
    slot = jnp.arange(N_BATCH, dtype=jnp.int32)[:, None, None] * CAPT + rank
    column = jnp.broadcast_to(jnp.arange(N_SEQ, dtype=jnp.int32)[None, :, None], owners.shape)
    stored = jnp.zeros((N_BATCH, N_SEQ, N_BATCH * CAPT, TROWS, D), jnp.bfloat16)
    stored = stored.at[owners, column, slot].set(residual)
    return (encoded.reshape(TOKENS, D), stored.reshape(N_BATCH, N_SEQ, N_BATCH * CAPT * TROWS, D))
```

```python
import functools
import math

import jax
import jax.numpy as jnp
import numpy as np
from jax import lax
from jax.experimental import pallas as pl
from jax.experimental.pallas import tpu as pltpu
from jax.sharding import PartitionSpec as P

H = 12
D = 768
FF = 3072
DOC_LEN = 8192
BAND = 256
CAP = 2
TROWS = 128
LPO = 64
NSEQ = 32
SDEV = 1024
BLK = 32
LEAD = 512
SPAN = NSEQ * SDEV
CH = 256
WIN = CH + 2 * BAND
FC = 256

norm_eps = 1e-06
LOG2E = math.log2(math.e)
FAR = -1e32
MIB = 1 << 20

ANY = pl.BlockSpec(memory_space=pl.ANY)
VMEM = pl.BlockSpec(memory_space=pltpu.VMEM)
SMEM = pl.BlockSpec(memory_space=pltpu.SMEM)
F32 = jnp.float32
BF16 = jnp.bfloat16


def head_slopes(heads):
    base = 2 ** int(np.floor(np.log2(heads)))
    first = [2.0 ** (-8.0 * (i + 1) / base) for i in range(base)]
    extra = [2.0 ** (-4.0 * (i + 1) / base) for i in range(2 * (heads - base))][0::2]
    return np.asarray(first + extra, np.float32)


def iota(shape, dim):
    return lax.broadcasted_iota(jnp.int32, shape, dim)


def dot(a, b):
    return jnp.dot(a, b, preferred_element_type=F32)


def pack_kernel(dest, packed, buffer, count, sems):
    def clear(i, _):
        count[i] = 0
        return 0

    lax.fori_loop(0, NSEQ, clear, 0)

    def copy_of(j, slot):
        return pltpu.make_async_copy(
            packed.at[pl.ds(pl.multiple_of(j * BLK, BLK), BLK)], buffer.at[slot], sems.at[j]
        )

    def send(j, _):
        owner = lax.shift_right_logical(dest[j], 5)
        rank = count[owner]
        count[owner] = rank + 1
        copy_of(j, owner * CAP + rank).start()
        return 0

    lax.fori_loop(0, BLK, send, 0)

    def finish(j, _):
        copy_of(j, 0).wait()
        return 0

    lax.fori_loop(0, BLK, finish, 0)


def pack(packed, dest):
    return pl.pallas_call(
        pack_kernel,
        out_shape=jax.ShapeDtypeStruct((NSEQ * CAP, BLK, D), BF16),
        in_specs=[SMEM, ANY],
        out_specs=ANY,
        scratch_shapes=[pltpu.SMEM((NSEQ,), jnp.int32), pltpu.SemaphoreType.DMA((BLK,))],
        name="pack_blocks",
    )(dest, packed)


def edge_kernel(src, received, head, tail, sems):
    copies = []
    per = BAND // BLK
    for q in range(per):
        copies.append(
            pltpu.make_async_copy(
                received.at[src[q]], head.at[pl.ds(q * BLK, BLK)], sems.at[q]
            )
        )
        copies.append(
            pltpu.make_async_copy(
                received.at[src[SDEV // BLK - per + q]],
                tail.at[pl.ds(q * BLK, BLK)],
                sems.at[per + q],
            )
        )
    for c in copies:
        c.start()
    for c in copies:
        c.wait()


def edges(src, received):
    shape = jax.ShapeDtypeStruct((BAND, D), BF16)
    return pl.pallas_call(
        edge_kernel,
        out_shape=(shape, shape),
        in_specs=[SMEM, ANY],
        out_specs=(ANY, ANY),
        scratch_shapes=[pltpu.SemaphoreType.DMA((2 * BAND // BLK,))],
        name="shard_edges",
    )(src, received)


def doc_bounds(info, doc_len, start):
    u0 = info[0] + LEAD + start
    doc = lax.shift_right_logical(u0, 13)
    base = doc * DOC_LEN
    length = doc_len[doc]
    low = jnp.maximum(0, LEAD - base)
    high = jnp.minimum(length, SPAN + LEAD - base)
    return u0 - base, length, low, high


def reach_table(info, doc_len, start):
    rel, _, low, high = doc_bounds(info, doc_len, start)
    j = iota((CH, WIN), 1)
    dist = jnp.abs(iota((CH, WIN), 0) + BAND - j)
    key = rel - BAND + j
    keep = (dist <= BAND) & (((key >= low) & (key < high)) | (dist == 0))
    return jnp.where(keep, -dist.astype(F32), FAR)


def layer_norm(v, gain, shift):
    centre = jnp.mean(v, axis=-1, keepdims=True)
    v = v - centre
    spread = jnp.mean(v * v, axis=-1, keepdims=True)
    return v * lax.rsqrt(spread + norm_eps) * gain + shift


def gelu(x):
    z = jnp.abs(x)
    t = 1.0 / (1.0 + z * (0.3275911 * math.sqrt(0.5)))
    p = t * (0.5 * 1.061405429) + (0.5 * -1.453152027)
    p = p * t + (0.5 * 1.421413741)
    p = p * t + (0.5 * -0.284496736)
    p = p * t + (0.5 * 0.254829592)
    q = p * t * jnp.exp2(x * x * (-0.5 * LOG2E))
    return jnp.maximum(x, 0.0) - z * q


def attend_pair(pair, chunks, qref, qrows, kvref, reach, slopes, att):
    lanes = pl.ds(pl.multiple_of(pair * 128, 128), 128)
    vlanes = pl.ds(pl.multiple_of(D + pair * 128, 128), 128)
    left = iota((CH, 128), 1) < 64
    ones = jnp.ones((WIN, 128), BF16)
    for n, c in enumerate(chunks):
        q = qref[pl.ds(qrows[n], CH), lanes]
        window = pl.ds(c * CH - kvref[1], WIN)
        k = kvref[0][window, lanes]
        v = jnp.concatenate([kvref[0][window, vlanes], ones], axis=1)
        halves = []
        for side in range(2):
            mine = left if side == 0 else jnp.logical_not(left)
            s = lax.dot_general(
                jnp.where(mine, q, jnp.zeros_like(q)),
                k,
                (((1,), (1,)), ((), ())),
                preferred_element_type=F32,
            )
            s = s + slopes[2 * pair + side] * reach[n]
            s = s - jnp.max(s, axis=-1, keepdims=True)
            o = dot(jnp.exp2(s).astype(BF16), v)
            halves.append(o[:, :128] / o[:, 128:])
        att[pl.ds(n * CH, CH), lanes] = jnp.where(left, halves[0], halves[1]).astype(BF16)


def tail_of_layer(chunks, x_of, att, first, active, w_out, w_glu, w_down, vecs, waits):
    b_out, g1, s1, b_down, g2, s2 = vecs
    rows = len(chunks) * CH
    waits[0]()
    mixed = dot(att[...], w_out[...]) + b_out[...] + x_of().astype(F32)
    first[...] = layer_norm(mixed, g1[...], s1[...]).astype(BF16)
    waits[1]()

    def part(i, _):
        cols = pl.ds(pl.multiple_of(i * FC, FC), FC)
        up = pl.ds(pl.multiple_of(FF + i * FC, FC), FC)
        f = first[...]
        active[:, cols] = (gelu(dot(f, w_glu[:, cols])) * dot(f, w_glu[:, up])).astype(BF16)
        return 0

    lax.fori_loop(0, FF // FC, part, 0)
    waits[2]()
    second = dot(active[...], w_down[...]) + b_down[...] + first[...].astype(F32)
    return layer_norm(second, g2[...], s2[...]).astype(BF16)


def pool_tile(info, doc_len, lists, chunk, enc, centroids):
    rel, length, _, _ = doc_bounds(info, doc_len, chunk * CH)
    r = iota((TROWS, CH), 0)
    i = iota((TROWS, CH), 1)
    scale = jnp.where(length - rel - 2 * r >= 2, 0.5, 1.0)
    mine = (lax.shift_right_logical(i, 1) == r) & (rel + i < length)
    pooled = dot(jnp.where(mine, scale, 0.0).astype(BF16), enc)
    pick = (iota((TROWS, centroids.shape[0]), 1) == lists[chunk]).astype(BF16)
    return (pooled - dot(pick, centroids[...])).astype(BF16)


def start_all(copies):
    for c in copies:
        c.start()


def mid_kernel(
    src, info, doc_len, lists, slopes,
    received, w_qkv_h, w_out_h, w_glu_h, w_down_h,
    b_qkv, b_out, g1, s1, b_down, g2, s2, centroids,
    enc_h, q_h, kv_h, tiles,
    x, w_qkv, w_out, w_glu, w_down, qs, kvs, att, first, active, reach, enc, wsem, xsem, osem,
):
    weights = [
        pltpu.make_async_copy(h, v, wsem.at[i])
        for i, (h, v) in enumerate(
            [(w_qkv_h, w_qkv), (w_out_h, w_out), (w_glu_h, w_glu), (w_down_h, w_down)]
        )
    ]
    blocks = [
        pltpu.make_async_copy(received.at[src[q]], x.at[pl.ds(q * BLK, BLK)], xsem.at[q])
        for q in range(SDEV // BLK)
    ]
    start_all(blocks)
    start_all(weights)
    chunks = (1, 2)
    for n, c in enumerate(chunks):
        reach[n] = reach_table(info, doc_len, c * CH)
    for b in blocks:
        b.wait()
    weights[0].wait()
    qs[...] = ((dot(x[...], w_qkv[:, :D]) + b_qkv[:, :D]) * (LOG2E / 8.0)).astype(BF16)
    kvs[...] = (dot(x[...], w_qkv[:, D:]) + b_qkv[:, D:]).astype(BF16)
    outs = [
        pltpu.make_async_copy(qs, q_h, osem.at[0]),
        pltpu.make_async_copy(kvs, kv_h, osem.at[1]),
    ]
    start_all(outs)

    def pairs(pair, _):
        attend_pair(pair, chunks, qs, (CH, 2 * CH), (kvs, BAND), reach, slopes, att)
        return 0

    lax.fori_loop(0, H // 2, pairs, 0)
    enc[...] = tail_of_layer(
        chunks, lambda: x[pl.ds(CH, 2 * CH)], att, first, active, w_out, w_glu, w_down,
        (b_out, g1, s1, b_down, g2, s2), [w.wait for w in weights[1:]],
    )
    last = pltpu.make_async_copy(enc, enc_h.at[pl.ds(CH, 2 * CH)], osem.at[2])
    last.start()
    for n, c in enumerate(chunks):
        tiles[n] = pool_tile(info, doc_len, lists, c, enc[pl.ds(n * CH, CH)], centroids)
    for o in outs + [last]:
        o.wait()


def edge_layer_kernel(
    src, info, doc_len, lists, slopes,
    received, before, after, q_h, kv_h, enc_in, w_qkv_h, w_out_h, w_glu_h, w_down_h,
    b_qkv, b_out, g1, s1, b_down, g2, s2, centroids,
    enc_h, tiles,
    x, halo, w_kv, w_out, w_glu, w_down, qs, kvs, att, first, active, reach, enc, wsem, xsem, osem,
):
    weights = [
        pltpu.make_async_copy(h, v, wsem.at[i])
        for i, (h, v) in enumerate(
            [
                (w_qkv_h.at[:, pl.ds(D, 2 * D)], w_kv),
                (w_out_h, w_out),
                (w_glu_h, w_glu),
                (w_down_h, w_down),
            ]
        )
    ]
    per = CH // BLK
    total = SDEV // BLK
    blocks = [
        pltpu.make_async_copy(
            received.at[src[q if q < per else total - 2 * per + q]],
            x.at[pl.ds(q * BLK, BLK)],
            xsem.at[q],
        )
        for q in range(2 * per)
    ]
    loads = [
        pltpu.make_async_copy(before, halo.at[pl.ds(0, BAND)], osem.at[0]),
        pltpu.make_async_copy(after, halo.at[pl.ds(BAND, BAND)], osem.at[1]),
    ]
    own = [
        pltpu.make_async_copy(q_h.at[pl.ds(0, CH)], qs.at[pl.ds(0, CH)], osem.at[2]),
        pltpu.make_async_copy(q_h.at[pl.ds(SDEV - CH, CH)], qs.at[pl.ds(CH, CH)], osem.at[3]),
        pltpu.make_async_copy(kv_h, kvs.at[pl.ds(BAND, SDEV)], osem.at[4]),
    ]
    start_all(loads)
    weights[0].start()
    start_all(own)
    start_all(blocks)
    start_all(weights[1:])
    chunks = (0, 3)
    for n, c in enumerate(chunks):
        reach[n] = reach_table(info, doc_len, c * CH)
    for c in loads:
        c.wait()
    weights[0].wait()
    sides = (dot(halo[...], w_kv[...]) + b_qkv[:, D:]).astype(BF16)
    kvs[pl.ds(0, BAND)] = sides[:BAND]
    kvs[pl.ds(BAND + SDEV, BAND)] = sides[BAND:]
    for c in own:
        c.wait()

    def pairs(pair, _):
        attend_pair(pair, chunks, qs, (0, CH), (kvs, 0), reach, slopes, att)
        return 0

    lax.fori_loop(0, H // 2, pairs, 0)
    for b in blocks:
        b.wait()
    enc[...] = tail_of_layer(
        chunks, lambda: x[...], att, first, active, w_out, w_glu, w_down,
        (b_out, g1, s1, b_down, g2, s2), [w.wait for w in weights[1:]],
    )
    last = [
        pltpu.make_async_copy(enc.at[pl.ds(0, CH)], enc_h.at[pl.ds(0, CH)], osem.at[5]),
        pltpu.make_async_copy(enc.at[pl.ds(CH, CH)], enc_h.at[pl.ds(SDEV - CH, CH)], osem.at[6]),
    ]
    start_all(last)
    for n, c in enumerate(chunks):
        tiles[n] = pool_tile(info, doc_len, lists, c, enc[pl.ds(n * CH, CH)], centroids)
    for o in last:
        o.wait()


def dma(*shape):
    return pltpu.SemaphoreType.DMA(shape)


def common_scratch():
    return [
        pltpu.VMEM((2 * CH, D), BF16),
        pltpu.VMEM((2 * CH, D), BF16),
        pltpu.VMEM((2 * CH, FF), BF16),
        pltpu.VMEM((2, CH, WIN), F32),
        pltpu.VMEM((2 * CH, D), BF16),
    ]


def mid_layer(src, info, doc_len, lists, slopes, received, ws, vecs):
    return pl.pallas_call(
        mid_kernel,
        out_shape=(
            jax.ShapeDtypeStruct((SDEV, D), BF16),
            jax.ShapeDtypeStruct((SDEV, D), BF16),
            jax.ShapeDtypeStruct((SDEV, 2 * D), BF16),
            jax.ShapeDtypeStruct((2, TROWS, D), BF16),
        ),
        in_specs=[SMEM] * 5 + [ANY] * 5 + [VMEM] * 8,
        out_specs=(ANY, ANY, ANY, VMEM),
        scratch_shapes=[
            pltpu.VMEM((SDEV, D), BF16),
            pltpu.VMEM((D, 3 * D), BF16),
            pltpu.VMEM((D, D), BF16),
            pltpu.VMEM((D, 2 * FF), BF16),
            pltpu.VMEM((FF, D), BF16),
            pltpu.VMEM((SDEV, D), BF16),
            pltpu.VMEM((SDEV, 2 * D), BF16),
        ]
        + common_scratch()
        + [dma(4), dma(SDEV // BLK), dma(3)],
        compiler_params=pltpu.CompilerParams(vmem_limit_bytes=56 * MIB),
        cost_estimate=pl.CostEstimate(
            flops=14_000_000_000, bytes_accessed=30_000_000, transcendentals=8_000_000
        ),
        name="mid_layer",
    )(src, info, doc_len, lists, slopes, received, *ws, *vecs)


def edge_layer(src, info, doc_len, lists, slopes, received, before, after, q, kv, enc, ws, vecs):
    return pl.pallas_call(
        edge_layer_kernel,
        out_shape=(
            jax.ShapeDtypeStruct((SDEV, D), BF16),
            jax.ShapeDtypeStruct((2, TROWS, D), BF16),
        ),
        in_specs=[SMEM] * 5 + [ANY] * 10 + [VMEM] * 8,
        out_specs=(ANY, VMEM),
        input_output_aliases={10: 0},
        scratch_shapes=[
            pltpu.VMEM((2 * CH, D), BF16),
            pltpu.VMEM((2 * BAND, D), BF16),
            pltpu.VMEM((D, 2 * D), BF16),
            pltpu.VMEM((D, D), BF16),
            pltpu.VMEM((D, 2 * FF), BF16),
            pltpu.VMEM((FF, D), BF16),
            pltpu.VMEM((2 * CH, D), BF16),
            pltpu.VMEM((SDEV + 2 * BAND, 2 * D), BF16),
        ]
        + common_scratch()
        + [dma(4), dma(2 * CH // BLK), dma(7)],
        compiler_params=pltpu.CompilerParams(vmem_limit_bytes=56 * MIB),
        cost_estimate=pl.CostEstimate(
            flops=12_000_000_000, bytes_accessed=30_000_000, transcendentals=8_000_000
        ),
        name="edge_layer",
    )(src, info, doc_len, lists, slopes, received, before, after, q, kv, enc, *ws, *vecs)


def store_kernel(pick, a, b, zeros, out, sems):
    copies = []
    for slot in range(8):
        dst = out.at[pl.ds(slot * TROWS, TROWS)]
        code = pick[slot]
        which = jnp.maximum(code, 0)

        @pl.when(code < 0)
        def _():
            pltpu.make_async_copy(zeros, dst, sems.at[slot]).start()

        @pl.when((code >= 0) & (lax.rem(which, 4) < 2))
        def _():
            n = lax.div(which, 4) * 2 + lax.rem(which, 4)
            pltpu.make_async_copy(a.at[n], dst, sems.at[slot]).start()

        @pl.when((code >= 0) & (lax.rem(which, 4) >= 2))
        def _():
            n = lax.div(which, 4) * 2 + lax.rem(which, 4) - 2
            pltpu.make_async_copy(b.at[n], dst, sems.at[slot]).start()

        copies.append(pltpu.make_async_copy(zeros, dst, sems.at[slot]))
    for c in copies:
        c.wait()


def store(pick, a, b):
    return pl.pallas_call(
        store_kernel,
        out_shape=jax.ShapeDtypeStruct((8 * TROWS, D), BF16),
        in_specs=[SMEM, ANY, ANY, VMEM],
        out_specs=ANY,
        scratch_shapes=[dma(8)],
        name="store_tiles",
    )(pick, a, b, jnp.zeros((TROWS, D), BF16))


def arrival_slots(dests, me):
    mine = (dests // NSEQ) == me
    order = jnp.arange(BLK, dtype=jnp.int32)
    before = (order[:, None] < order[None, :]).astype(F32)
    rank = jnp.dot(mine.astype(F32), before).astype(jnp.int32)
    slot = jnp.arange(NSEQ, dtype=jnp.int32)[:, None] * CAP + rank
    place = jnp.where(mine, dests % NSEQ, -1).reshape(1, -1)
    hit = place == jnp.arange(NSEQ, dtype=jnp.int32)[:, None]
    return jnp.sum(jnp.where(hit, slot.reshape(1, -1), 0), axis=1)


def stored_slots(lists, me):
    owner = lists // LPO
    mine = owner == me
    order = jnp.arange(4, dtype=jnp.int32)
    rank = jnp.sum(
        (mine[:, None, :] & (order[None, None, :] < order[None, :, None])).astype(jnp.int32), axis=2
    )
    place = jnp.asarray([2, 0, 1, 3], jnp.int32)
    code = jnp.arange(4, dtype=jnp.int32)[:, None] * 4 + place[None, :]
    slots = jnp.arange(2, dtype=jnp.int32)
    hit = mine[:, None, :] & (rank[:, None, :] == slots[None, :, None])
    return (jnp.sum(jnp.where(hit, code[:, None, :] + 1, 0), axis=2) - 1).reshape(-1)


def on_device(
    packed, block_dest, doc_len, w_qkv, b_qkv, w_out, b_out, norm1_gain, norm1_shift,
    w_glu, w_down, b_down, norm2_gain, norm2_shift, centroids, tile_list,
):
    seq_here = lax.axis_index("seq")
    batch_here = lax.axis_index("batch")
    dests = lax.all_gather(block_dest, "seq", axis=0)
    lists = lax.all_gather(tile_list, "batch", axis=0)
    received = lax.all_to_all(
        pack(packed, block_dest), "seq", split_axis=0, concat_axis=0, tiled=True
    )
    src = arrival_slots(dests, seq_here)
    pick = stored_slots(lists, batch_here)
    info = (seq_here * SDEV).astype(jnp.int32).reshape(1)
    slopes = jnp.asarray(head_slopes(H) * np.float32(LOG2E))
    row = lambda v: v.reshape(1, -1)
    ws = (w_qkv, w_out, w_glu, w_down)
    vecs = (
        row(b_qkv), row(b_out), row(norm1_gain), row(norm1_shift),
        row(b_down), row(norm2_gain), row(norm2_shift), centroids,
    )
    head, tail = edges(src, received)
    up = [(i, i + 1) for i in range(NSEQ - 1)]
    down = [(j, i) for i, j in up]
    before = lax.ppermute(tail, "seq", up)
    after = lax.ppermute(head, "seq", down)
    enc, q, kv, tiles_a = mid_layer(src, info, doc_len, tile_list, slopes, received, ws, vecs)
    all_a = lax.all_gather(tiles_a, "batch", axis=0, tiled=True)
    enc, tiles_b = edge_layer(
        src, info, doc_len, tile_list, slopes, received, before, after, q, kv, enc, ws, vecs
    )
    all_b = lax.all_gather(tiles_b, "batch", axis=0, tiled=True)
    stored = store(pick, all_a, all_b)
    return enc, stored.reshape(1, 1, 8 * TROWS, D)


def solution(mesh):
    return jax.shard_map(
        on_device,
        mesh=mesh,
        in_specs=(
            P(("batch", "seq"), None),
            P(("batch", "seq")),
            P("batch"),
            P(), P(), P(), P(), P(), P(), P(), P(), P(), P(), P(), P(),
            P(("batch", "seq")),
        ),
        out_specs=(P(("batch", "seq"), None), P("batch", "seq", None, None)),
        check_vma=False,
    )
```

```python
import functools
import math

import jax
import jax.numpy as jnp
import numpy as np
from jax import lax
from jax.experimental import pallas as pl
from jax.experimental.pallas import tpu as pltpu
from jax.sharding import PartitionSpec as P

H = 12
D = 768
FF = 3072
DOC_LEN = 8192
BAND = 256
CAP = 2
TROWS = 128
LPO = 64
NSEQ = 32
BATCHES = 4
SDEV = 1024
BLK = 32
LEAD = 512
SPAN = NSEQ * SDEV
CH = 256
WIN = CH + 2 * BAND
GROUPS = D // 128
PIECES = CAP * GROUPS * BLK
LABEL_ROWS = 16
FC = 768
PAIR_UNROLL = 6
FF_UNROLL = 4

norm_eps = 1e-06
LOG2E = math.log2(math.e)
FAR = -1e32
MIB = 1 << 20
KERNEL_VMEM = 48 * MIB
SMALL_VMEM = 8 * MIB

ANY = pl.BlockSpec(memory_space=pl.ANY)
VMEM = pl.BlockSpec(memory_space=pltpu.VMEM)
SMEM = pl.BlockSpec(memory_space=pltpu.SMEM)
F32 = jnp.float32
BF16 = jnp.bfloat16


def head_slopes(heads):
    base = 2 ** int(np.floor(np.log2(heads)))
    first = [2.0 ** (-8.0 * (i + 1) / base) for i in range(base)]
    extra = [2.0 ** (-4.0 * (i + 1) / base) for i in range(2 * (heads - base))][0::2]
    return np.asarray(first + extra, np.float32)


def iota(shape, dim):
    return lax.broadcasted_iota(jnp.int32, shape, dim)


def dot(a, b):
    return jnp.dot(a, b, preferred_element_type=F32)


def piece(rank, group):
    return pl.ds(pl.multiple_of((rank * GROUPS + group) * BLK, BLK), BLK)


def pack_kernel(dest, packed, parts, count):
    def clear(i, _):
        count[i] = 0
        parts[i, pl.ds(PIECES, LABEL_ROWS)] = jnp.zeros((LABEL_ROWS, 128), BF16)
        return 0

    lax.fori_loop(0, NSEQ, clear, 0)
    lane = iota((LABEL_ROWS, 128), 1)

    def send(j, _):
        owner = lax.shift_right_logical(dest[j], 5)
        rank = count[owner]
        count[owner] = rank + 1
        rows = pl.ds(pl.multiple_of(j * BLK, BLK), BLK)
        for g in range(GROUPS):
            parts[owner, piece(rank, g)] = packed[rows, g * 128 : (g + 1) * 128]
        label = (dest[j] & (NSEQ - 1)) + 1
        old = parts[owner, pl.ds(PIECES, LABEL_ROWS)]
        new = jnp.where(lane == rank, label.astype(F32), old.astype(F32))
        parts[owner, pl.ds(PIECES, LABEL_ROWS)] = new.astype(BF16)
        return 0

    lax.fori_loop(0, BLK, send, 0)


def pack(packed, dest):
    return pl.pallas_call(
        pack_kernel,
        out_shape=jax.ShapeDtypeStruct((NSEQ, PIECES + LABEL_ROWS, 128), BF16),
        in_specs=[SMEM, VMEM],
        out_specs=VMEM,
        scratch_shapes=[pltpu.SMEM((NSEQ,), jnp.int32)],
        compiler_params=pltpu.CompilerParams(vmem_limit_bytes=SMALL_VMEM),
        name="pack_blocks",
    )(dest, packed)


def place_kernel(received, x, head, tail, vector, labels, sem):
    found = received[:, pl.ds(PIECES, LABEL_ROWS)].astype(F32)
    vector[...] = jnp.max(found, axis=1).astype(jnp.int32)
    copy = pltpu.make_async_copy(vector, labels, sem)
    copy.start()
    copy.wait()

    def fetch(source, _):
        for rank in range(CAP):
            label = labels[source, rank]

            @pl.when(label > 0)
            def _():
                rows = pl.ds(pl.multiple_of((label - 1) * BLK, BLK), BLK)
                for g in range(GROUPS):
                    x[rows, g * 128 : (g + 1) * 128] = received[source, piece(rank, g)]

        return 0

    lax.fori_loop(0, NSEQ, fetch, 0)
    head[...] = x[:BAND]
    tail[...] = x[SDEV - BAND :]


def place(received):
    return pl.pallas_call(
        place_kernel,
        out_shape=[jax.ShapeDtypeStruct((n, D), BF16) for n in (SDEV, BAND, BAND)],
        in_specs=[VMEM],
        out_specs=[VMEM] * 3,
        scratch_shapes=[
            pltpu.VMEM((NSEQ, 128), jnp.int32),
            pltpu.SMEM((NSEQ, 128), jnp.int32),
            dma(),
        ],
        compiler_params=pltpu.CompilerParams(vmem_limit_bytes=SMALL_VMEM),
        name="place_blocks",
    )(received)


def doc_bounds(info, doc_len, start):
    u0 = info[0] + LEAD + start
    doc = lax.shift_right_logical(u0, 13)
    base = doc * DOC_LEN
    length = doc_len[doc]
    low = jnp.maximum(0, LEAD - base)
    high = jnp.minimum(length, SPAN + LEAD - base)
    return u0 - base, length, low, high


def reach_table(info, doc_len, start):
    rel, _, low, high = doc_bounds(info, doc_len, start)
    j = iota((CH, WIN), 1)
    dist = jnp.abs(iota((CH, WIN), 0) + BAND - j)
    key = rel - BAND + j
    keep = (dist <= BAND) & (((key >= low) & (key < high)) | (dist == 0))
    return jnp.where(keep, -dist.astype(F32), FAR)


def layer_norm(v, gain, shift):
    centre = jnp.mean(v, axis=-1, keepdims=True)
    v = v - centre
    spread = jnp.mean(v * v, axis=-1, keepdims=True)
    return v * lax.rsqrt(spread + norm_eps) * gain + shift


def gelu(x):
    z = jnp.abs(x)
    t = 1.0 / (1.0 + z * (0.3275911 * math.sqrt(0.5)))
    p = t * (0.5 * 1.061405429) + (0.5 * -1.453152027)
    p = p * t + (0.5 * 1.421413741)
    p = p * t + (0.5 * -0.284496736)
    p = p * t + (0.5 * 0.254829592)
    q = p * t * jnp.exp2(x * x * (-0.5 * LOG2E))
    return jnp.maximum(x, 0.0) - z * q


def attend_pair(pair, chunks, qref, qrows, kvref, reach, slopes, att):
    lanes = pl.ds(pl.multiple_of(pair * 128, 128), 128)
    vlanes = pl.ds(pl.multiple_of(D + pair * 128, 128), 128)
    left = iota((CH, 128), 1) < 64
    ones = jnp.ones((WIN, 128), BF16)
    for n, c in enumerate(chunks):
        q = qref[pl.ds(qrows[n], CH), lanes]
        window = pl.ds(c * CH - kvref[1], WIN)
        k = kvref[0][window, lanes]
        v = jnp.concatenate([kvref[0][window, vlanes], ones], axis=1)
        halves = []
        for side in range(2):
            mine = left if side == 0 else jnp.logical_not(left)
            s = lax.dot_general(
                jnp.where(mine, q, jnp.zeros_like(q)),
                k,
                (((1,), (1,)), ((), ())),
                preferred_element_type=F32,
            )
            s = s + slopes[2 * pair + side] * reach[n]
            s = s - jnp.max(s, axis=-1, keepdims=True)
            o = dot(jnp.exp2(s).astype(BF16), v)
            halves.append(o[:, :128] / o[:, 128:])
        att[pl.ds(n * CH, CH), lanes] = jnp.where(left, halves[0], halves[1]).astype(BF16)


def pool_tile(info, doc_len, lists, chunk, enc, centroids):
    rel, length, _, _ = doc_bounds(info, doc_len, chunk * CH)
    r = iota((TROWS, CH), 0)
    i = iota((TROWS, CH), 1)
    scale = jnp.where(length - rel - 2 * r >= 2, 0.5, 1.0)
    mine = (lax.shift_right_logical(i, 1) == r) & (rel + i < length)
    pooled = dot(jnp.where(mine, scale, 0.0).astype(BF16), enc)
    pick = (iota((TROWS, centroids.shape[0]), 1) == lists[chunk]).astype(BF16)
    return (pooled - dot(pick, centroids[...])).astype(BF16)


def start_all(copies):
    for c in copies:
        c.start()


def wait_all(copies):
    for c in copies:
        c.wait()


def layer_of(chunks, att, x_rows, first, active, ws, loads, vecs):
    b_out, g1, s1, b_down, g2, s2 = vecs
    w_out, w_glu, w_down = ws
    loads[0].wait()
    mixed = dot(att[...], w_out[...]) + b_out[...] + x_rows.astype(F32)
    first[...] = layer_norm(mixed, g1[...], s1[...]).astype(BF16)
    loads[1].wait()

    def part(i, _):
        cols = pl.ds(pl.multiple_of(i * FC, FC), FC)
        up = pl.ds(pl.multiple_of(FF + i * FC, FC), FC)
        f = first[...]
        active[:, cols] = (gelu(dot(f, w_glu[:, cols])) * dot(f, w_glu[:, up])).astype(BF16)
        return 0

    lax.fori_loop(0, FF // FC, part, 0, unroll=FF_UNROLL)
    loads[2].wait()
    second = dot(active[...], w_down[...]) + b_down[...] + first[...].astype(F32)
    return layer_norm(second, g2[...], s2[...]).astype(BF16)


def loads_of(sources, targets, sems):
    return [pltpu.make_async_copy(s, t, sems.at[i]) for i, (s, t) in enumerate(zip(sources, targets))]


def mid_kernel(
    info, doc_len, lists, slopes, head,
    w_qkv_h, w_out_h, w_glu_h, w_down_h, x,
    b_qkv, b_out, g1, s1, b_down, g2, s2, centroids,
    enc_h, qs, kvs, tiles,
    w_qkv, w_out, w_glu, w_down, att, first, active, reach, enc, wsem, osem,
):
    chunks = (1, 2)
    ws = (w_out, w_glu, w_down)
    heads = pltpu.make_async_copy(w_qkv_h, w_qkv, wsem.at[3])
    heads.start()
    loads = loads_of((w_out_h, w_glu_h, w_down_h), ws, wsem)
    for n, c in enumerate(chunks):
        reach[n] = reach_table(info, doc_len, c * CH)
    heads.wait()
    start_all(loads)
    qs[...] = ((dot(x[...], w_qkv[:, :D]) + b_qkv[:, :D]) * (LOG2E / 8.0)).astype(BF16)
    kvs[...] = (dot(x[...], w_qkv[:, D:]) + b_qkv[:, D:]).astype(BF16)

    def pairs(pair, _):
        attend_pair(pair, chunks, qs, (CH, 2 * CH), (kvs, BAND), reach, slopes, att)
        return 0

    lax.fori_loop(0, H // 2, pairs, 0, unroll=PAIR_UNROLL)
    enc[...] = layer_of(
        chunks, att, x[pl.ds(CH, 2 * CH)], first, active, ws, loads,
        (b_out, g1, s1, b_down, g2, s2),
    )
    last = pltpu.make_async_copy(enc, enc_h.at[pl.ds(CH, 2 * CH)], osem.at[2])
    last.start()
    for n, c in enumerate(chunks):
        tiles[n] = pool_tile(info, doc_len, lists, c, enc[pl.ds(n * CH, CH)], centroids)
    last.wait()


def edge_kernel(
    chunk, info, doc_len, lists, slopes,
    enc_in, w_qkv_h, w_out_h, w_glu_h, w_down_h, halo, x, q, kv,
    b_qkv, b_out, g1, s1, b_down, g2, s2, centroids,
    *rest,
):
    enc_h, tile, kvs, w_kv, w_out, w_glu, w_down = rest[-14:-7]
    att, first, active, reach, enc, wsem, osem = rest[-7:]
    ws = (w_out, w_glu, w_down)
    sides_load = pltpu.make_async_copy(w_qkv_h.at[:, pl.ds(D, 2 * D)], w_kv, wsem.at[3])
    sides_load.start()
    loads = loads_of((w_out_h, w_glu_h, w_down_h), ws, wsem)
    start = chunk * CH
    reach[0] = reach_table(info, doc_len, start)
    sides_load.wait()
    start_all(loads)
    sides = (dot(halo[...], w_kv[...]) + b_qkv[:, D:]).astype(BF16)
    if chunk == 0:
        kvs[pl.ds(0, BAND)] = sides
        kvs[pl.ds(BAND, WIN - BAND)] = kv[pl.ds(0, WIN - BAND)]
    else:
        kvs[pl.ds(0, WIN - BAND)] = kv[pl.ds(start - BAND, WIN - BAND)]
        kvs[pl.ds(WIN - BAND, BAND)] = sides

    def pairs(pair, _):
        attend_pair(pair, (chunk,), q, (start,), (kvs, start), reach, slopes, att)
        return 0

    lax.fori_loop(0, H // 2, pairs, 0, unroll=PAIR_UNROLL)
    enc[...] = layer_of(
        (chunk,), att, x[pl.ds(start, CH)], first, active, ws, loads,
        (b_out, g1, s1, b_down, g2, s2),
    )
    last = pltpu.make_async_copy(enc, enc_h.at[pl.ds(start, CH)], osem.at[2])
    last.start()
    tile[...] = pool_tile(info, doc_len, lists, chunk, enc[...], centroids)
    last.wait()


def dma(*shape):
    return pltpu.SemaphoreType.DMA(shape)


def common_scratch(rows):
    return [
        pltpu.VMEM((D, D), BF16),
        pltpu.VMEM((D, 2 * FF), BF16),
        pltpu.VMEM((FF, D), BF16),
        pltpu.VMEM((rows, D), BF16),
        pltpu.VMEM((rows, D), BF16),
        pltpu.VMEM((rows, FF), BF16),
        pltpu.VMEM((rows // CH, CH, WIN), F32),
        pltpu.VMEM((rows, D), BF16),
        dma(4),
        dma(3),
    ]


def mid_layer(info, doc_len, lists, slopes, head, x, ws, vecs):
    return pl.pallas_call(
        mid_kernel,
        out_shape=(
            jax.ShapeDtypeStruct((SDEV, D), BF16),
            jax.ShapeDtypeStruct((SDEV, D), BF16),
            jax.ShapeDtypeStruct((SDEV, 2 * D), BF16),
            jax.ShapeDtypeStruct((2, TROWS, D), BF16),
        ),
        in_specs=[SMEM] * 4 + [ANY] * 5 + [VMEM] * 9,
        out_specs=(ANY, VMEM, VMEM, VMEM),
        scratch_shapes=[pltpu.VMEM((D, 3 * D), BF16)] + common_scratch(2 * CH),
        compiler_params=pltpu.CompilerParams(vmem_limit_bytes=KERNEL_VMEM),
        cost_estimate=pl.CostEstimate(
            flops=14_000_000_000, bytes_accessed=30_000_000, transcendentals=8_000_000
        ),
        name="mid_layer",
    )(info, doc_len, lists, slopes, head, *ws, x, *vecs)


def edge_layer(chunk, info, doc_len, lists, slopes, halo, x, q, kv, enc, ws, vecs, after=()):
    return pl.pallas_call(
        functools.partial(edge_kernel, chunk),
        out_shape=(
            jax.ShapeDtypeStruct((SDEV, D), BF16),
            jax.ShapeDtypeStruct((TROWS, D), BF16),
        ),
        in_specs=[SMEM] * 4 + [ANY] * 5 + [VMEM] * 12 + [ANY] * len(after),
        out_specs=(ANY, VMEM),
        input_output_aliases={4: 0},
        scratch_shapes=[pltpu.VMEM((WIN, 2 * D), BF16), pltpu.VMEM((D, 2 * D), BF16)]
        + common_scratch(CH),
        compiler_params=pltpu.CompilerParams(vmem_limit_bytes=KERNEL_VMEM),
        cost_estimate=pl.CostEstimate(
            flops=6_000_000_000, bytes_accessed=15_000_000, transcendentals=4_000_000
        ),
        name="edge_layer_%d" % chunk,
    )(info, doc_len, lists, slopes, enc, *ws, halo, x, q, kv, *vecs, *after)


def slot_of(here, lists, k, tile):
    device = (here[0] + BATCHES - k) & (BATCHES - 1)
    mine = [lax.shift_right_logical(lists[k * 4 + t], 6) == here[0] for t in range(4)]
    counts = [m.astype(jnp.int32) for m in mine]
    rank = sum(counts[:tile], jnp.int32(0))
    row = pl.multiple_of((device * CAP + jnp.minimum(rank, CAP - 1)) * TROWS, TROWS)
    return mine[tile], row, device, sum(counts, jnp.int32(0))


def store_kernel(here, lists, *refs):
    pairs, singles, out, sems = refs[:4], refs[4:8], refs[8], refs[9]
    moves = []
    for k in range(BATCHES):
        for t, source in ((1, pairs[k].at[0]), (2, pairs[k].at[1]), (0, singles[k])):
            mine, row, _, _ = slot_of(here, lists, k, t)
            dst = out.at[pl.ds(row, TROWS)]
            moves.append((mine, pltpu.make_async_copy(source, dst, sems.at[len(moves)])))
        _, _, device, total = slot_of(here, lists, k, 0)
        for r in range(CAP):

            @pl.when(total <= r)
            def _():
                row = pl.multiple_of((device * CAP + r) * TROWS, TROWS)
                out[pl.ds(row, TROWS)] = jnp.zeros((TROWS, D), BF16)

    for go, copy in moves:
        pl.when(go)(copy.start)
    for go, copy in moves:
        pl.when(go)(copy.wait)


def store(here, lists, pairs, singles):
    return pl.pallas_call(
        store_kernel,
        out_shape=jax.ShapeDtypeStruct((BATCHES * CAP * TROWS, D), BF16),
        in_specs=[SMEM] * 2 + [ANY] * 8,
        out_specs=VMEM,
        scratch_shapes=[dma(12)],
        compiler_params=pltpu.CompilerParams(vmem_limit_bytes=SMALL_VMEM),
        name="store_tiles",
    )(here, lists, *pairs, *singles)


def store_last_kernel(here, lists, *refs):
    singles, out, sems = refs[:4], refs[5], refs[6]
    moves = []
    for k in range(BATCHES):
        mine, row, _, _ = slot_of(here, lists, k, 3)
        dst = out.at[pl.ds(row, TROWS)]
        moves.append((mine, pltpu.make_async_copy(singles[k], dst, sems.at[k])))
    for go, copy in moves:
        pl.when(go)(copy.start)
    for go, copy in moves:
        pl.when(go)(copy.wait)


def store_last(here, lists, singles, stored):
    return pl.pallas_call(
        store_last_kernel,
        out_shape=jax.ShapeDtypeStruct(stored.shape, BF16),
        in_specs=[SMEM] * 2 + [VMEM] * 4 + [ANY],
        out_specs=ANY,
        input_output_aliases={6: 0},
        scratch_shapes=[dma(4)],
        compiler_params=pltpu.CompilerParams(vmem_limit_bytes=SMALL_VMEM),
        name="store_last_tile",
    )(here, lists, *singles, stored)


def on_device(
    packed, block_dest, doc_len, w_qkv, b_qkv, w_out, b_out, norm1_gain, norm1_shift,
    w_glu, w_down, b_down, norm2_gain, norm2_shift, centroids, tile_list,
):
    seq_here = lax.axis_index("seq")
    batch_here = lax.axis_index("batch")

    def from_batch(v):
        turns = [[(i, (i + k) % BATCHES) for i in range(BATCHES)] for k in range(1, BATCHES)]
        return [v] + [lax.ppermute(v, "batch", t) for t in turns]

    received = lax.all_to_all(
        pack(packed, block_dest), "seq", split_axis=0, concat_axis=0, tiled=True
    )
    lists = jnp.concatenate(from_batch(tile_list))
    info = (seq_here * SDEV).astype(jnp.int32).reshape(1)
    here = batch_here.astype(jnp.int32).reshape(1)
    slopes = jnp.asarray(head_slopes(H) * np.float32(LOG2E))
    row = lambda v: v.reshape(1, -1)
    ws = (w_qkv, w_out, w_glu, w_down)
    vecs = (
        row(b_qkv), row(b_out), row(norm1_gain), row(norm1_shift),
        row(b_down), row(norm2_gain), row(norm2_shift), centroids,
    )
    x, head, tail = place(received)
    up = [(i, i + 1) for i in range(NSEQ - 1)]
    down = [(j, i) for i, j in up]
    before = lax.ppermute(tail, "seq", up)
    after = lax.ppermute(head, "seq", down)
    enc, q, kv, pair = mid_layer(info, doc_len, lists, slopes, head, x, ws, vecs)
    pairs = from_batch(pair)
    enc, tile_0 = edge_layer(0, info, doc_len, lists, slopes, before, x, q, kv, enc, ws, vecs)
    firsts = from_batch(tile_0)
    enc, tile_3 = edge_layer(
        3, info, doc_len, lists, slopes, after, x, q, kv, enc, ws, vecs, after=pairs[1:]
    )
    tile_3, *firsts = lax.optimization_barrier((tile_3, *firsts))
    lasts = from_batch(tile_3)
    stored = store(here, lists, pairs, firsts)
    stored = store_last(here, lists, lasts, stored)
    return enc, stored.reshape(1, 1, BATCHES * CAP * TROWS, D)


def solution(mesh):
    return jax.shard_map(
        on_device,
        mesh=mesh,
        in_specs=(
            P(("batch", "seq"), None),
            P(("batch", "seq")),
            P("batch"),
            P(), P(), P(), P(), P(), P(), P(), P(), P(), P(), P(), P(),
            P(("batch", "seq")),
        ),
        out_specs=(P(("batch", "seq"), None), P("batch", "seq", None, None)),
        check_vma=False,
    )
```

```python
import functools
import math

import jax
import jax.numpy as jnp
import numpy as np
from jax import lax
from jax.experimental import pallas as pl
from jax.experimental.pallas import tpu as pltpu
from jax.sharding import PartitionSpec as P

H = 12
D = 768
FF = 3072
DOC_LEN = 8192
BAND = 256
CAP = 2
TROWS = 128
LPO = 64
NSEQ = 32
BATCHES = 4
SDEV = 1024
BLK = 32
LEAD = 512
SPAN = NSEQ * SDEV
CH = 256
WIN = CH + 2 * BAND
GROUPS = D // 128
PIECES = CAP * GROUPS * BLK
LABEL_ROWS = 16
FC = 768

norm_eps = 1e-06
LOG2E = math.log2(math.e)
FAR = -1e32
MIB = 1 << 20
KERNEL_VMEM = 36 * MIB
SMALL_VMEM = 8 * MIB
PACK_VMEM = 56 * MIB

ANY = pl.BlockSpec(memory_space=pl.ANY)
VMEM = pl.BlockSpec(memory_space=pltpu.VMEM)
SMEM = pl.BlockSpec(memory_space=pltpu.SMEM)
F32 = jnp.float32
BF16 = jnp.bfloat16


def head_slopes(heads):
    base = 2 ** int(np.floor(np.log2(heads)))
    first = [2.0 ** (-8.0 * (i + 1) / base) for i in range(base)]
    extra = [2.0 ** (-4.0 * (i + 1) / base) for i in range(2 * (heads - base))][0::2]
    return np.asarray(first + extra, np.float32)


def iota(shape, dim):
    return lax.broadcasted_iota(jnp.int32, shape, dim)


def dot(a, b):
    return jnp.dot(a, b, preferred_element_type=F32)


def piece(rank, group):
    return pl.ds(pl.multiple_of((rank * GROUPS + group) * BLK, BLK), BLK)


def pack_kernel(dest, packed_h, parts, packed, count, sem):
    load = pltpu.make_async_copy(packed_h, packed, sem)
    load.start()

    def clear(i, _):
        count[i] = 0
        parts[i, pl.ds(PIECES, LABEL_ROWS)] = jnp.zeros((LABEL_ROWS, 128), BF16)
        return 0

    lax.fori_loop(0, NSEQ, clear, 0)
    lane = iota((LABEL_ROWS, 128), 1)
    load.wait()

    def send(j, _):
        owner = lax.shift_right_logical(dest[j], 5)
        rank = count[owner]
        count[owner] = rank + 1
        rows = pl.ds(pl.multiple_of(j * BLK, BLK), BLK)
        for g in range(GROUPS):
            parts[owner, piece(rank, g)] = packed[rows, g * 128 : (g + 1) * 128]
        label = (dest[j] & (NSEQ - 1)) + 1
        old = parts[owner, pl.ds(PIECES, LABEL_ROWS)]
        new = jnp.where(lane == rank, label.astype(F32), old.astype(F32))
        parts[owner, pl.ds(PIECES, LABEL_ROWS)] = new.astype(BF16)
        return 0

    lax.fori_loop(0, BLK, send, 0)


def pack(packed, dest):
    return pl.pallas_call(
        pack_kernel,
        out_shape=jax.ShapeDtypeStruct((NSEQ, PIECES + LABEL_ROWS, 128), BF16),
        in_specs=[SMEM, ANY],
        out_specs=VMEM,
        scratch_shapes=[pltpu.VMEM((SDEV, D), BF16), pltpu.SMEM((NSEQ,), jnp.int32), dma()],
        compiler_params=pltpu.CompilerParams(vmem_limit_bytes=PACK_VMEM),
        name="pack_blocks",
    )(dest, packed)


def project_kernel(
    received, w_qkv_h, b_qkv,
    x_h, q_h, kv_h, head, tail,
    x, q, kv, w_qkv, vector, labels, sem, wsem, osem,
):
    columns = [pl.ds(D, D), pl.ds(2 * D, D), pl.ds(0, D)]
    loads = [
        pltpu.make_async_copy(w_qkv_h.at[:, c], w_qkv.at[:, c], wsem.at[i])
        for i, c in enumerate(columns)
    ]
    start_all(loads)
    found = received[:, pl.ds(PIECES, LABEL_ROWS)].astype(F32)
    vector[...] = jnp.max(found, axis=1).astype(jnp.int32)
    copy = pltpu.make_async_copy(vector, labels, sem)
    copy.start()
    copy.wait()

    def fetch(source, _):
        for rank in range(CAP):
            label = labels[source, rank]

            @pl.when(label > 0)
            def _():
                rows = pl.ds(pl.multiple_of((label - 1) * BLK, BLK), BLK)
                for g in range(GROUPS):
                    x[rows, g * 128 : (g + 1) * 128] = received[source, piece(rank, g)]

        return 0

    lax.fori_loop(0, NSEQ, fetch, 0)
    outs = [
        pltpu.make_async_copy(x, x_h, osem.at[0]),
        pltpu.make_async_copy(kv, kv_h, osem.at[1]),
        pltpu.make_async_copy(kv.at[pl.ds(0, BAND)], head, osem.at[2]),
        pltpu.make_async_copy(kv.at[pl.ds(SDEV - BAND, BAND)], tail, osem.at[3]),
        pltpu.make_async_copy(q, q_h, osem.at[4]),
    ]
    outs[0].start()
    for i in range(2):
        loads[i].wait()
        part = dot(x[...], w_qkv[:, columns[i]]) + b_qkv[:, columns[i]]
        kv[:, pl.ds(i * D, D)] = part.astype(BF16)
    start_all(outs[1:4])
    loads[2].wait()
    q[...] = ((dot(x[...], w_qkv[:, :D]) + b_qkv[:, :D]) * (LOG2E / 8.0)).astype(BF16)
    outs[4].start()
    wait_all(outs)


def project(received, w_qkv, b_qkv):
    shapes = [(SDEV, D), (SDEV, D), (SDEV, 2 * D), (BAND, 2 * D), (BAND, 2 * D)]
    return pl.pallas_call(
        project_kernel,
        out_shape=[jax.ShapeDtypeStruct(shape, BF16) for shape in shapes],
        in_specs=[VMEM, ANY, VMEM],
        out_specs=[ANY] * 5,
        scratch_shapes=[
            pltpu.VMEM((SDEV, D), BF16),
            pltpu.VMEM((SDEV, D), BF16),
            pltpu.VMEM((SDEV, 2 * D), BF16),
            pltpu.VMEM((D, 3 * D), BF16),
            pltpu.VMEM((NSEQ, 128), jnp.int32),
            pltpu.SMEM((NSEQ, 128), jnp.int32),
            dma(),
            dma(3),
            dma(5),
        ],
        compiler_params=pltpu.CompilerParams(vmem_limit_bytes=28 * MIB),
        name="project_tokens",
    )(received, w_qkv, b_qkv)


def doc_bounds(info, doc_len, start):
    u0 = info[0] + LEAD + start
    doc = lax.shift_right_logical(u0, 13)
    base = doc * DOC_LEN
    length = doc_len[doc]
    low = jnp.maximum(0, LEAD - base)
    high = jnp.minimum(length, SPAN + LEAD - base)
    return u0 - base, length, low, high


def reach_table(info, doc_len, start):
    rel, _, low, high = doc_bounds(info, doc_len, start)
    j = iota((CH, WIN), 1)
    dist = jnp.abs(iota((CH, WIN), 0) + BAND - j)
    key = rel - BAND + j
    keep = (dist <= BAND) & (((key >= low) & (key < high)) | (dist == 0))
    return jnp.where(keep, -dist.astype(F32), FAR)


def layer_norm(v, gain, shift):
    centre = jnp.mean(v, axis=-1, keepdims=True)
    v = v - centre
    spread = jnp.mean(v * v, axis=-1, keepdims=True)
    return v * lax.rsqrt(spread + norm_eps) * gain + shift


def gelu(x):
    z = jnp.abs(x)
    t = 1.0 / (1.0 + z * (0.3275911 * math.sqrt(0.5)))
    p = t * (0.5 * 1.061405429) + (0.5 * -1.453152027)
    p = p * t + (0.5 * 1.421413741)
    p = p * t + (0.5 * -0.284496736)
    p = p * t + (0.5 * 0.254829592)
    q = p * t * jnp.exp2(x * x * (-0.5 * LOG2E))
    return jnp.maximum(x, 0.0) - z * q


def attend_pair(pair, chunks, q, window, reach, slopes, att):
    lanes = pl.ds(pair * 128, 128)
    vlanes = pl.ds(D + pair * 128, 128)
    left = iota((CH, 128), 1) < 64
    ones = jnp.ones((WIN, 128), BF16)
    for n, c in enumerate(chunks):
        mine = q[pl.ds(c * CH, CH), lanes]
        k = window(c, lanes)
        v = jnp.concatenate([window(c, vlanes), ones], axis=1)
        halves = []
        for side in range(2):
            here = left if side == 0 else jnp.logical_not(left)
            s = lax.dot_general(
                jnp.where(here, mine, jnp.zeros_like(mine)),
                k,
                (((1,), (1,)), ((), ())),
                preferred_element_type=F32,
            )
            s = s + slopes[2 * pair + side] * reach[n]
            s = s - jnp.max(s, axis=-1, keepdims=True)
            o = dot(jnp.exp2(s).astype(BF16), v)
            halves.append(o[:, :128] / o[:, 128:])
        att[pl.ds(n * CH, CH), lanes] = jnp.where(left, halves[0], halves[1]).astype(BF16)


def pool_tile(info, doc_len, lists, chunk, enc, centroids):
    rel, length, _, _ = doc_bounds(info, doc_len, chunk * CH)
    r = iota((TROWS, CH), 0)
    i = iota((TROWS, CH), 1)
    scale = jnp.where(length - rel - 2 * r >= 2, 0.5, 1.0)
    mine = (lax.shift_right_logical(i, 1) == r) & (rel + i < length)
    pooled = dot(jnp.where(mine, scale, 0.0).astype(BF16), enc)
    pick = (iota((TROWS, centroids.shape[0]), 1) == lists[chunk]).astype(BF16)
    return (pooled - dot(pick, centroids[...])).astype(BF16)


def start_all(copies):
    for c in copies:
        c.start()


def wait_all(copies):
    for c in copies:
        c.wait()


def layer_of(att, x_rows, first, active, ws, loads, vecs):
    w_out, w_glu, w_down = ws
    b_out, g1, s1, b_down, g2, s2 = vecs
    loads[0].wait()
    mixed = dot(att[...], w_out[...]) + b_out[...] + x_rows.astype(F32)
    first[...] = layer_norm(mixed, g1[...], s1[...]).astype(BF16)
    loads[1].wait()
    for i in range(FF // FC):
        cols = pl.ds(i * FC, FC)
        up = pl.ds(FF + i * FC, FC)
        f = first[...]
        active[:, cols] = (gelu(dot(f, w_glu[:, cols])) * dot(f, w_glu[:, up])).astype(BF16)
    loads[2].wait()
    second = dot(active[...], w_down[...]) + b_down[...] + first[...].astype(F32)
    return layer_norm(second, g2[...], s2[...]).astype(BF16)


def loads_of(sources, targets, sems):
    return [pltpu.make_async_copy(s, t, sems.at[i]) for i, (s, t) in enumerate(zip(sources, targets))]


def layer_kernel(
    chunks, before, info, doc_len, lists, slopes,
    enc_in, w_out_h, w_glu_h, w_down_h, x, q, kv, *rest,
):
    halo = None if before is None else rest[0]
    b_out, g1, s1, b_down, g2, s2, centroids = rest[:7] if halo is None else rest[1:8]
    enc_h, tiles, w_out, w_glu, w_down, att, first, active, reach, enc, wsem, osem = rest[-12:]
    ws = (w_out, w_glu, w_down)
    loads = loads_of((w_out_h, w_glu_h, w_down_h), ws, wsem)
    start_all(loads)
    start = chunks[0] * CH
    rows = len(chunks) * CH
    for n, c in enumerate(chunks):
        reach[n] = reach_table(info, doc_len, c * CH)

    def window(c, lanes):
        if halo is None:
            return kv[pl.ds(c * CH - BAND, WIN), lanes]
        own = kv[pl.ds(0 if before else c * CH - BAND, WIN - BAND), lanes]
        return jnp.concatenate([halo[:, lanes], own] if before else [own, halo[:, lanes]], axis=0)

    for pair in range(H // 2):
        attend_pair(pair, chunks, q, window, reach, slopes, att)
    enc[...] = layer_of(
        att, x[pl.ds(start, rows)], first, active, ws, loads, (b_out, g1, s1, b_down, g2, s2)
    )
    last = pltpu.make_async_copy(enc, enc_h.at[pl.ds(start, rows)], osem)
    last.start()
    for n, c in enumerate(chunks):
        tiles[n] = pool_tile(info, doc_len, lists, c, enc[pl.ds(n * CH, CH)], centroids)
    last.wait()


def dma(*shape):
    return pltpu.SemaphoreType.DMA(shape)


def layer(chunks, scalars, enc, ws, x, q, kv, vecs, halo=None, before=None, after=()):
    rows = len(chunks) * CH
    halos = () if halo is None else (halo,)
    rest = (x, q, kv) + halos + vecs
    return pl.pallas_call(
        functools.partial(layer_kernel, chunks, before),
        out_shape=(
            jax.ShapeDtypeStruct((SDEV, D), BF16),
            jax.ShapeDtypeStruct((len(chunks), TROWS, D), BF16),
        ),
        in_specs=[SMEM] * 4 + [ANY] * 4 + [VMEM] * len(rest) + [ANY] * len(after),
        out_specs=(ANY, VMEM),
        input_output_aliases={} if halo is None else {4: 0},
        scratch_shapes=[
            pltpu.VMEM((D, D), BF16),
            pltpu.VMEM((D, 2 * FF), BF16),
            pltpu.VMEM((FF, D), BF16),
            pltpu.VMEM((rows, D), BF16),
            pltpu.VMEM((rows, D), BF16),
            pltpu.VMEM((rows, FF), BF16),
            pltpu.VMEM((len(chunks), CH, WIN), F32),
            pltpu.VMEM((rows, D), BF16),
            dma(3),
            dma(),
        ],
        compiler_params=pltpu.CompilerParams(vmem_limit_bytes=KERNEL_VMEM),
        cost_estimate=pl.CostEstimate(
            flops=12_000_000 * rows, bytes_accessed=20_000_000, transcendentals=16_000 * rows
        ),
        name="layer_chunk_%d" % chunks[0],
    )(*scalars, enc, *ws, *rest, *after)


def slot_of(here, lists, k, tile):
    device = (here[0] + BATCHES - k) & (BATCHES - 1)
    mine = [lax.shift_right_logical(lists[k * 4 + t], 6) == here[0] for t in range(4)]
    counts = [m.astype(jnp.int32) for m in mine]
    rank = sum(counts[:tile], jnp.int32(0))
    row = pl.multiple_of((device * CAP + jnp.minimum(rank, CAP - 1)) * TROWS, TROWS)
    return mine[tile], row, device, sum(counts, jnp.int32(0))


def store_kernel(here, lists, *refs):
    pairs, singles, out, sems = refs[:4], refs[4:8], refs[8], refs[9]
    moves = []
    for k in range(BATCHES):
        for t, source in ((1, pairs[k].at[0]), (2, pairs[k].at[1]), (0, singles[k].at[0])):
            mine, row, _, _ = slot_of(here, lists, k, t)
            dst = out.at[pl.ds(row, TROWS)]
            moves.append((mine, pltpu.make_async_copy(source, dst, sems.at[len(moves)])))
        _, _, device, total = slot_of(here, lists, k, 0)
        for r in range(CAP):

            @pl.when(total <= r)
            def _():
                row = pl.multiple_of((device * CAP + r) * TROWS, TROWS)
                out[pl.ds(row, TROWS)] = jnp.zeros((TROWS, D), BF16)

    for go, copy in moves:
        pl.when(go)(copy.start)
    for go, copy in moves:
        pl.when(go)(copy.wait)


def store(here, lists, pairs, singles):
    return pl.pallas_call(
        store_kernel,
        out_shape=jax.ShapeDtypeStruct((BATCHES * CAP * TROWS, D), BF16),
        in_specs=[SMEM] * 2 + [ANY] * 8,
        out_specs=VMEM,
        scratch_shapes=[dma(12)],
        compiler_params=pltpu.CompilerParams(vmem_limit_bytes=SMALL_VMEM),
        name="store_tiles",
    )(here, lists, *pairs, *singles)


def store_last_kernel(here, lists, *refs):
    singles, out, sems = refs[:4], refs[5], refs[6]
    moves = []
    for k in range(BATCHES):
        mine, row, _, _ = slot_of(here, lists, k, 3)
        dst = out.at[pl.ds(row, TROWS)]
        moves.append((mine, pltpu.make_async_copy(singles[k].at[0], dst, sems.at[k])))
    for go, copy in moves:
        pl.when(go)(copy.start)
    for go, copy in moves:
        pl.when(go)(copy.wait)


def store_last(here, lists, singles, stored):
    return pl.pallas_call(
        store_last_kernel,
        out_shape=jax.ShapeDtypeStruct(stored.shape, BF16),
        in_specs=[SMEM] * 2 + [VMEM] * 4 + [ANY],
        out_specs=ANY,
        input_output_aliases={6: 0},
        scratch_shapes=[dma(4)],
        compiler_params=pltpu.CompilerParams(vmem_limit_bytes=SMALL_VMEM),
        name="store_last_tile",
    )(here, lists, *singles, stored)


def on_device(
    packed, block_dest, doc_len, w_qkv, b_qkv, w_out, b_out, norm1_gain, norm1_shift,
    w_glu, w_down, b_down, norm2_gain, norm2_shift, centroids, tile_list,
):
    seq_here = lax.axis_index("seq")
    batch_here = lax.axis_index("batch")

    def from_batch(v):
        turns = [[(i, (i + k) % BATCHES) for i in range(BATCHES)] for k in range(1, BATCHES)]
        return [v] + [lax.ppermute(v, "batch", t) for t in turns]

    received = lax.all_to_all(
        pack(packed, block_dest), "seq", split_axis=0, concat_axis=0, tiled=True
    )
    lists = jnp.concatenate(from_batch(tile_list))
    info = (seq_here * SDEV).astype(jnp.int32).reshape(1)
    here = batch_here.astype(jnp.int32).reshape(1)
    slopes = jnp.asarray(head_slopes(H) * np.float32(LOG2E))
    row = lambda v: v.reshape(1, -1)
    ws = (w_out, w_glu, w_down)
    vecs = (
        row(b_out), row(norm1_gain), row(norm1_shift),
        row(b_down), row(norm2_gain), row(norm2_shift), centroids,
    )
    x, q, kv, head, tail = project(received, w_qkv, row(b_qkv))
    up = [(i, i + 1) for i in range(NSEQ - 1)]
    down = [(j, i) for i, j in up]
    before = lax.ppermute(tail, "seq", up)
    after = lax.ppermute(head, "seq", down)
    scalars = (info, doc_len, lists, slopes)
    enc, pair = layer((1, 2), scalars, x, ws, x, q, kv, vecs)
    pairs = from_batch(pair)
    enc, tile_0 = layer((0,), scalars, enc, ws, x, q, kv, vecs, halo=before, before=True)
    firsts = from_batch(tile_0)
    enc, tile_3 = layer(
        (3,), scalars, enc, ws, x, q, kv, vecs, halo=after, before=False, after=pairs[1:]
    )
    tile_3, *firsts = lax.optimization_barrier((tile_3, *firsts))
    lasts = from_batch(tile_3)
    stored = store(here, lists, pairs, firsts)
    stored = store_last(here, lists, lasts, stored)
    return enc, stored.reshape(1, 1, BATCHES * CAP * TROWS, D)


def solution(mesh):
    return jax.shard_map(
        on_device,
        mesh=mesh,
        in_specs=(
            P(("batch", "seq"), None),
            P(("batch", "seq")),
            P("batch"),
            P(), P(), P(), P(), P(), P(), P(), P(), P(), P(), P(), P(),
            P(("batch", "seq")),
        ),
        out_specs=(P(("batch", "seq"), None), P("batch", "seq", None, None)),
        check_vma=False,
    )
```

```python
import functools
import math

import jax
import jax.numpy as jnp
import numpy as np
from jax import lax
from jax.experimental import pallas as pl
from jax.experimental.pallas import tpu as pltpu
from jax.sharding import PartitionSpec as P

H = 12
D = 768
FF = 3072
DOC_LEN = 8192
BAND = 256
CAP = 2
TROWS = 128
LPO = 64
NSEQ = 32
BATCHES = 4
SDEV = 1024
BLK = 32
LEAD = 512
SPAN = NSEQ * SDEV
CH = 256
WIN = CH + 2 * BAND
HALF = CH // 2
KEYS = HALF + 2 * BAND
GROUPS = D // 128
PIECES = CAP * GROUPS * BLK
LABEL_ROWS = 16
LOADS = 4
FC = 768

norm_eps = 1e-06
LOG2E = math.log2(math.e)
FAR = -1e32
MIB = 1 << 20
KERNEL_VMEM = 36 * MIB
SMALL_VMEM = 8 * MIB
PACK_VMEM = 56 * MIB
PROJECT_VMEM = 46 * MIB

ANY = pl.BlockSpec(memory_space=pl.ANY)
VMEM = pl.BlockSpec(memory_space=pltpu.VMEM)
SMEM = pl.BlockSpec(memory_space=pltpu.SMEM)
F32 = jnp.float32
BF16 = jnp.bfloat16


def head_slopes(heads):
    base = 2 ** int(np.floor(np.log2(heads)))
    first = [2.0 ** (-8.0 * (i + 1) / base) for i in range(base)]
    extra = [2.0 ** (-4.0 * (i + 1) / base) for i in range(2 * (heads - base))][0::2]
    return np.asarray(first + extra, np.float32)


def iota(shape, dim):
    return lax.broadcasted_iota(jnp.int32, shape, dim)


def dot(a, b):
    return jnp.dot(a, b, preferred_element_type=F32)


def piece(rank, group):
    return pl.ds(pl.multiple_of((rank * GROUPS + group) * BLK, BLK), BLK)


def pack_kernel(dest, packed_h, parts, packed, staged, labels, count, load_sems, sems, label_sem):
    step = SDEV // LOADS
    loads = [
        pltpu.make_async_copy(
            packed_h.at[pl.ds(i * step, step)], packed.at[pl.ds(i * step, step)], load_sems.at[i]
        )
        for i in range(LOADS)
    ]
    start_all(loads)
    labels[...] = jnp.zeros_like(labels)

    def clear(i, _):
        count[i] = 0
        return 0

    lax.fori_loop(0, NSEQ, clear, 0)
    lane = iota((LABEL_ROWS, 128), 1)

    def copy_of(j, owner, rank):
        rows = pl.ds(pl.multiple_of(rank * GROUPS * BLK, GROUPS * BLK), GROUPS * BLK)
        return pltpu.make_async_copy(staged.at[j], parts.at[owner, rows], sems.at[j])

    def send(j, _):
        owner = lax.shift_right_logical(dest[j], 5)
        rank = count[owner]
        count[owner] = rank + 1
        rows = pl.ds(pl.multiple_of(j * BLK, BLK), BLK)
        for g in range(GROUPS):
            staged[j, g * BLK : (g + 1) * BLK] = packed[rows, g * 128 : (g + 1) * 128]
        copy_of(j, owner, rank).start()
        label = (dest[j] & (NSEQ - 1)) + 1
        new = jnp.where(lane == rank, label.astype(F32), labels[owner].astype(F32))
        labels[owner] = new.astype(BF16)
        return 0

    per = BLK // LOADS
    for i in range(LOADS):
        loads[i].wait()
        lax.fori_loop(i * per, (i + 1) * per, send, 0)
    last = pltpu.make_async_copy(labels, parts.at[:, pl.ds(PIECES, LABEL_ROWS)], label_sem)
    last.start()

    def finish(j, _):
        copy_of(j, 0, 0).wait()
        return 0

    lax.fori_loop(0, BLK, finish, 0)
    last.wait()


def pack(packed, dest):
    return pl.pallas_call(
        pack_kernel,
        out_shape=jax.ShapeDtypeStruct((NSEQ, PIECES + LABEL_ROWS, 128), BF16),
        in_specs=[SMEM, ANY],
        out_specs=ANY,
        scratch_shapes=[
            pltpu.VMEM((SDEV, D), BF16),
            pltpu.VMEM((BLK, GROUPS * BLK, 128), BF16),
            pltpu.VMEM((NSEQ, LABEL_ROWS, 128), BF16),
            pltpu.SMEM((NSEQ,), jnp.int32),
            dma(LOADS),
            dma(BLK),
            dma(),
        ],
        compiler_params=pltpu.CompilerParams(vmem_limit_bytes=PACK_VMEM),
        name="pack_blocks",
    )(dest, packed)


def project_kernel(
    received, w_qkv_h, b_qkv,
    x, q, kv, head, tail,
    w_qkv, vector, labels, sem, wsem,
):
    columns = [pl.ds(D, D), pl.ds(2 * D, D), pl.ds(0, D)]
    loads = [
        pltpu.make_async_copy(w_qkv_h.at[:, c], w_qkv.at[:, c], wsem.at[i])
        for i, c in enumerate(columns)
    ]
    start_all(loads)
    found = received[:, pl.ds(PIECES, LABEL_ROWS)].astype(F32)
    vector[...] = jnp.max(found, axis=1).astype(jnp.int32)
    copy = pltpu.make_async_copy(vector, labels, sem)
    copy.start()
    copy.wait()

    def fetch(source, _):
        for rank in range(CAP):
            label = labels[source, rank]

            @pl.when(label > 0)
            def _():
                rows = pl.ds(pl.multiple_of((label - 1) * BLK, BLK), BLK)
                for g in range(GROUPS):
                    x[rows, g * 128 : (g + 1) * 128] = received[source, piece(rank, g)]

        return 0

    lax.fori_loop(0, NSEQ, fetch, 0)
    for i in range(2):
        loads[i].wait()
        part = dot(x[...], w_qkv[:, columns[i]]) + b_qkv[:, columns[i]]
        kv[:, pl.ds(i * D, D)] = part.astype(BF16)
        head[:, pl.ds(i * D, D)] = part[:BAND].astype(BF16)
        tail[:, pl.ds(i * D, D)] = part[SDEV - BAND :].astype(BF16)
    loads[2].wait()
    q[...] = ((dot(x[...], w_qkv[:, :D]) + b_qkv[:, :D]) * (LOG2E / 8.0)).astype(BF16)


def project(received, w_qkv, b_qkv):
    shapes = [(SDEV, D), (SDEV, D), (SDEV, 2 * D), (BAND, 2 * D), (BAND, 2 * D)]
    return pl.pallas_call(
        project_kernel,
        out_shape=[jax.ShapeDtypeStruct(shape, BF16) for shape in shapes],
        in_specs=[VMEM, ANY, VMEM],
        out_specs=[VMEM] * 5,
        scratch_shapes=[
            pltpu.VMEM((D, 3 * D), BF16),
            pltpu.VMEM((NSEQ, 128), jnp.int32),
            pltpu.SMEM((NSEQ, 128), jnp.int32),
            dma(),
            dma(3),
        ],
        compiler_params=pltpu.CompilerParams(vmem_limit_bytes=PROJECT_VMEM),
        name="project_tokens",
    )(received, w_qkv, b_qkv)


def doc_bounds(info, doc_len, start):
    u0 = info[0] + LEAD + start
    doc = lax.shift_right_logical(u0, 13)
    base = doc * DOC_LEN
    length = doc_len[doc]
    low = jnp.maximum(0, LEAD - base)
    high = jnp.minimum(length, SPAN + LEAD - base)
    return u0 - base, length, low, high


def reach_table(info, doc_len, start):
    rel, _, low, high = doc_bounds(info, doc_len, start)
    j = iota((CH, WIN), 1)
    dist = jnp.abs(iota((CH, WIN), 0) + BAND - j)
    key = rel - BAND + j
    keep = (dist <= BAND) & (((key >= low) & (key < high)) | (dist == 0))
    return jnp.where(keep, -dist.astype(F32), FAR)


def layer_norm(v, gain, shift):
    centre = jnp.mean(v, axis=-1, keepdims=True)
    v = v - centre
    spread = jnp.mean(v * v, axis=-1, keepdims=True)
    return v * lax.rsqrt(spread + norm_eps) * gain + shift


def gelu(x):
    z = jnp.abs(x)
    t = 1.0 / (1.0 + z * (0.3275911 * math.sqrt(0.5)))
    p = t * (0.5 * 1.061405429) + (0.5 * -1.453152027)
    p = p * t + (0.5 * 1.421413741)
    p = p * t + (0.5 * -0.284496736)
    p = p * t + (0.5 * 0.254829592)
    q = p * t * jnp.exp2(x * x * (-0.5 * LOG2E))
    return jnp.maximum(x, 0.0) - z * q


def attend_pair(pair, chunks, q, window, reach, slopes, att):
    lanes = pl.ds(pair * 128, 128)
    vlanes = pl.ds(D + pair * 128, 128)
    left = iota((CH, 128), 1) < 64
    ones = jnp.ones((WIN, 128), BF16)
    outside = jnp.zeros((HALF, WIN - KEYS), BF16)
    for n, c in enumerate(chunks):
        mine = q[pl.ds(c * CH, CH), lanes]
        none = jnp.zeros_like(mine)
        both = jnp.concatenate([jnp.where(left, mine, none), jnp.where(left, none, mine)], axis=0)
        scores = lax.dot_general(
            both, window(c, lanes), (((1,), (1,)), ((), ())), preferred_element_type=F32
        )
        probs = []
        for side in range(2):
            for half in range(2):
                row = half * HALF
                keys = slice(half * HALF, half * HALF + KEYS)
                s = scores[side * CH + row : side * CH + row + HALF, keys]
                s = s + slopes[2 * pair + side] * reach[n, row : row + HALF, keys]
                p = jnp.exp2(s - jnp.max(s, axis=-1, keepdims=True)).astype(BF16)
                probs.append(jnp.concatenate([outside, p] if half else [p, outside], axis=1))
        v = jnp.concatenate([window(c, vlanes), ones], axis=1)
        o = dot(jnp.concatenate(probs, axis=0), v)
        o = o[:, :128] / o[:, 128:]
        att[pl.ds(n * CH, CH), lanes] = jnp.where(left, o[:CH], o[CH:]).astype(BF16)


def pool_tile(info, doc_len, lists, chunk, enc, centroids):
    rel, length, _, _ = doc_bounds(info, doc_len, chunk * CH)
    r = iota((TROWS, CH), 0)
    i = iota((TROWS, CH), 1)
    scale = jnp.where(length - rel - 2 * r >= 2, 0.5, 1.0)
    mine = (lax.shift_right_logical(i, 1) == r) & (rel + i < length)
    pooled = dot(jnp.where(mine, scale, 0.0).astype(BF16), enc)
    pick = (iota((TROWS, centroids.shape[0]), 1) == lists[chunk]).astype(BF16)
    return (pooled - dot(pick, centroids[...])).astype(BF16)


def start_all(copies):
    for c in copies:
        c.start()


def wait_all(copies):
    for c in copies:
        c.wait()


def layer_of(att, x, start, first, active, enc, ws, loads, vecs):
    w_out, w_glu, w_down = ws
    b_out, g1, s1, b_down, g2, s2 = vecs
    count = att.shape[0]
    part = count // 2
    loads[0].wait()
    for r in range(0, count, part):
        rows = pl.ds(r, part)
        mixed = dot(att[rows], w_out[...]) + b_out[...] + x[pl.ds(start + r, part)].astype(F32)
        first[rows] = layer_norm(mixed, g1[...], s1[...]).astype(BF16)
    loads[1].wait()
    for i in range(FF // FC):
        cols = pl.ds(i * FC, FC)
        up = pl.ds(FF + i * FC, FC)
        f = first[...]
        active[:, cols] = (gelu(dot(f, w_glu[:, cols])) * dot(f, w_glu[:, up])).astype(BF16)
    loads[2].wait()
    for r in range(0, count, part):
        rows = pl.ds(r, part)
        second = dot(active[rows], w_down[...]) + b_down[...] + first[rows].astype(F32)
        enc[rows] = layer_norm(second, g2[...], s2[...]).astype(BF16)


def loads_of(sources, targets, sems):
    return [pltpu.make_async_copy(s, t, sems.at[i]) for i, (s, t) in enumerate(zip(sources, targets))]


def layer_kernel(
    chunks, before, info, doc_len, lists, slopes,
    enc_in, w_out_h, w_glu_h, w_down_h, x, q, kv, *rest,
):
    halo = None if before is None else rest[0]
    b_out, g1, s1, b_down, g2, s2, centroids = rest[:7] if halo is None else rest[1:8]
    enc_h, *tiles, w_out, w_glu, w_down, att, first, active, reach, enc, wsem, osem = rest[
        {None: 7, True: 9, False: 8}[before] :
    ]
    ws = (w_out, w_glu, w_down)
    loads = loads_of((w_out_h, w_glu_h, w_down_h), ws, wsem)
    start_all(loads)
    start = chunks[0] * CH
    rows = len(chunks) * CH
    for n, c in enumerate(chunks):
        reach[n] = reach_table(info, doc_len, c * CH)

    def window(c, lanes):
        if halo is None:
            return kv[pl.ds(c * CH - BAND, WIN), lanes]
        own = kv[pl.ds(0 if before else c * CH - BAND, WIN - BAND), lanes]
        return jnp.concatenate([halo[:, lanes], own] if before else [own, halo[:, lanes]], axis=0)

    for pair in range(H // 2):
        attend_pair(pair, chunks, q, window, reach, slopes, att)
    layer_of(att, x, start, first, active, enc, ws, loads, (b_out, g1, s1, b_down, g2, s2))
    last = pltpu.make_async_copy(enc, enc_h.at[pl.ds(start, rows)], osem)
    last.start()
    for n, c in enumerate(chunks):
        tile = pool_tile(info, doc_len, lists, c, enc[pl.ds(n * CH, CH)], centroids)
        if before:
            att[pl.ds(0, TROWS)] = tile
            send_tiles(info, lists, att.at[pl.ds(0, TROWS)], rest[8], tiles)
        else:
            tiles[0][n] = tile
    last.wait()


def send_tiles(info, lists, tile_0, tiles_12, groups):
    owners = [lax.shift_right_logical(lists[t], 6) for t in range(3)]
    for g in groups:
        g[...] = jnp.zeros_like(g)
    for t in range(3):
        rank = sum([(owners[e] == owners[t]).astype(jnp.int32) for e in range(t)], jnp.int32(0))
        turn = (owners[t] + BATCHES - info[1]) & (BATCHES - 1)
        for k, g in enumerate(groups):

            @pl.when(turn == k)
            def _():
                g[rank] = tile_0[...] if t == 0 else tiles_12[t - 1]


def dma(*shape):
    return pltpu.SemaphoreType.DMA(shape)


def layer(chunks, scalars, enc, ws, x, q, kv, vecs, halo=None, before=None, tiles_12=None):
    rows = len(chunks) * CH
    rest = (x, q, kv) + (() if halo is None else (halo,)) + vecs
    rest += () if tiles_12 is None else (tiles_12,)
    tiles = [(CAP, TROWS, D)] * BATCHES if before else [(len(chunks), TROWS, D)]
    return pl.pallas_call(
        functools.partial(layer_kernel, chunks, before),
        out_shape=(
            jax.ShapeDtypeStruct((SDEV, D), BF16),
            *[jax.ShapeDtypeStruct(shape, BF16) for shape in tiles],
        ),
        in_specs=[SMEM] * 4 + [ANY] * 4 + [VMEM] * len(rest),
        out_specs=(ANY,) + (VMEM,) * len(tiles),
        input_output_aliases={} if halo is None else {4: 0},
        scratch_shapes=[
            pltpu.VMEM((D, D), BF16),
            pltpu.VMEM((D, 2 * FF), BF16),
            pltpu.VMEM((FF, D), BF16),
            pltpu.VMEM((rows, D), BF16),
            pltpu.VMEM((rows, D), BF16),
            pltpu.VMEM((rows, FF), BF16),
            pltpu.VMEM((len(chunks), CH, WIN), F32),
            pltpu.VMEM((rows, D), BF16),
            dma(3),
            dma(),
        ],
        compiler_params=pltpu.CompilerParams(vmem_limit_bytes=KERNEL_VMEM),
        cost_estimate=pl.CostEstimate(
            flops=12_000_000 * rows, bytes_accessed=20_000_000, transcendentals=16_000 * rows
        ),
        name="layer_chunk_%d" % chunks[0],
    )(*scalars, enc, *ws, *rest)


def store_kernel(info, *refs):
    groups, out, sems = refs[:BATCHES], refs[BATCHES], refs[BATCHES + 1]
    moves = []
    for k in range(BATCHES):
        device = (info[1] + BATCHES - k) & (BATCHES - 1)
        for r in range(CAP):
            row = pl.multiple_of((device * CAP + r) * TROWS, TROWS)
            dst = out.at[pl.ds(row, TROWS)]
            moves.append(pltpu.make_async_copy(groups[k].at[r], dst, sems.at[k * CAP + r]))
    start_all(moves)
    wait_all(moves)


def store(info, groups):
    return pl.pallas_call(
        store_kernel,
        out_shape=jax.ShapeDtypeStruct((BATCHES * CAP * TROWS, D), BF16),
        in_specs=[SMEM] + [VMEM] * BATCHES,
        out_specs=ANY,
        scratch_shapes=[dma(BATCHES * CAP)],
        compiler_params=pltpu.CompilerParams(vmem_limit_bytes=SMALL_VMEM),
        name="store_tiles",
    )(info, *groups)


def store_last_kernel(info, lists, *refs):
    singles, out, sems = refs[:BATCHES], refs[BATCHES + 1], refs[BATCHES + 2]
    moves = []
    for k in range(BATCHES):
        device = (info[1] + BATCHES - k) & (BATCHES - 1)
        mine = [lax.shift_right_logical(lists[k * 4 + t], 6) == info[1] for t in range(4)]
        rank = sum([m.astype(jnp.int32) for m in mine[:3]], jnp.int32(0))
        row = pl.multiple_of((device * CAP + jnp.minimum(rank, CAP - 1)) * TROWS, TROWS)
        dst = out.at[pl.ds(row, TROWS)]
        moves.append((mine[3], pltpu.make_async_copy(singles[k].at[0], dst, sems.at[k])))
    for go, copy in moves:
        pl.when(go)(copy.start)
    for go, copy in moves:
        pl.when(go)(copy.wait)


def store_last(info, lists, singles, stored):
    return pl.pallas_call(
        store_last_kernel,
        out_shape=jax.ShapeDtypeStruct(stored.shape, BF16),
        in_specs=[SMEM] * 2 + [VMEM] * BATCHES + [ANY],
        out_specs=ANY,
        input_output_aliases={2 + BATCHES: 0},
        scratch_shapes=[dma(BATCHES)],
        compiler_params=pltpu.CompilerParams(vmem_limit_bytes=SMALL_VMEM),
        name="store_last_tile",
    )(info, lists, *singles, stored)


def on_device(
    packed, block_dest, doc_len, w_qkv, b_qkv, w_out, b_out, norm1_gain, norm1_shift,
    w_glu, w_down, b_down, norm2_gain, norm2_shift, centroids, tile_list,
):
    seq_here = lax.axis_index("seq")
    batch_here = lax.axis_index("batch")

    def from_batch(values):
        far = {}
        for k in (1, 3, 2):
            turn = [(i, (i + k) % BATCHES) for i in range(BATCHES)]
            far[k] = lax.ppermute(values[k], "batch", turn)
        return [values[0], far[1], far[2], far[3]]

    received = lax.all_to_all(
        pack(packed, block_dest), "seq", split_axis=0, concat_axis=0, tiled=True
    )
    lists = jnp.concatenate(from_batch([tile_list] * BATCHES))
    info = jnp.stack([seq_here * SDEV, batch_here]).astype(jnp.int32)
    slopes = jnp.asarray(head_slopes(H) * np.float32(LOG2E))
    row = lambda v: v.reshape(1, -1)
    ws = (w_out, w_glu, w_down)
    vecs = (
        row(b_out), row(norm1_gain), row(norm1_shift),
        row(b_down), row(norm2_gain), row(norm2_shift), centroids,
    )
    x, q, kv, head, tail = project(received, w_qkv, row(b_qkv))
    up = [(i, i + 1) for i in range(NSEQ - 1)]
    down = [(j, i) for i, j in up]
    before = lax.ppermute(tail, "seq", up)
    after = lax.ppermute(head, "seq", down)
    scalars = (info, doc_len, lists, slopes)
    enc, tiles_12 = layer((1, 2), scalars, x, ws, x, q, kv, vecs)
    enc, *groups = layer(
        (0,), scalars, enc, ws, x, q, kv, vecs, halo=before, before=True, tiles_12=tiles_12
    )
    groups = from_batch(groups)
    enc, tile_3 = layer((3,), scalars, enc, ws, x, q, kv, vecs, halo=after, before=False)
    tile_3, groups = lax.optimization_barrier((tile_3, groups))
    lasts = from_batch([tile_3] * BATCHES)
    stored = store_last(info, lists, lasts, store(info, groups))
    return enc, stored.reshape(1, 1, BATCHES * CAP * TROWS, D)


def solution(mesh):
    return jax.shard_map(
        on_device,
        mesh=mesh,
        in_specs=(
            P(("batch", "seq"), None),
            P(("batch", "seq")),
            P("batch"),
            P(), P(), P(), P(), P(), P(), P(), P(), P(), P(), P(), P(),
            P(("batch", "seq")),
        ),
        out_specs=(P(("batch", "seq"), None), P("batch", "seq", None, None)),
        check_vma=False,
    )
```

```python
import functools
import math

import jax
import jax.numpy as jnp
import numpy as np
from jax import lax
from jax.experimental import pallas as pl
from jax.experimental.pallas import tpu as pltpu
from jax.sharding import PartitionSpec as P

H = 12
D = 768
FF = 3072
DOC_LEN = 8192
BAND = 256
CAP = 2
TROWS = 128
LPO = 64
NSEQ = 32
BATCHES = 4
SDEV = 1024
BLK = 32
LEAD = 512
SPAN = NSEQ * SDEV
CH = 256
WIN = CH + 2 * BAND
HALF = CH // 2
KEYS = HALF + 2 * BAND
GROUPS = D // 128
PIECES = CAP * GROUPS * BLK
LABEL_ROWS = 16
LOADS = 4
FC = 768

norm_eps = 1e-06
LOG2E = math.log2(math.e)
FAR = -1e32
MIB = 1 << 20
KERNEL_VMEM = 36 * MIB
SMALL_VMEM = 8 * MIB
PACK_VMEM = 56 * MIB
PROJECT_VMEM = 46 * MIB

ANY = pl.BlockSpec(memory_space=pl.ANY)
VMEM = pl.BlockSpec(memory_space=pltpu.VMEM)
SMEM = pl.BlockSpec(memory_space=pltpu.SMEM)
F32 = jnp.float32
BF16 = jnp.bfloat16


def head_slopes(heads):
    base = 2 ** int(np.floor(np.log2(heads)))
    first = [2.0 ** (-8.0 * (i + 1) / base) for i in range(base)]
    extra = [2.0 ** (-4.0 * (i + 1) / base) for i in range(2 * (heads - base))][0::2]
    return np.asarray(first + extra, np.float32)


def iota(shape, dim):
    return lax.broadcasted_iota(jnp.int32, shape, dim)


def dot(a, b):
    return jnp.dot(a, b, preferred_element_type=F32)


def piece(rank, group):
    return pl.ds(pl.multiple_of((rank * GROUPS + group) * BLK, BLK), BLK)


def pack_kernel(dest, packed_h, parts, packed, staged, labels, count, load_sems, sems, label_sem):
    step = SDEV // LOADS
    loads = [
        pltpu.make_async_copy(
            packed_h.at[pl.ds(i * step, step)], packed.at[pl.ds(i * step, step)], load_sems.at[i]
        )
        for i in range(LOADS)
    ]
    start_all(loads)
    labels[...] = jnp.zeros_like(labels)

    def clear(i, _):
        count[i] = 0
        return 0

    lax.fori_loop(0, NSEQ, clear, 0)
    lane = iota((LABEL_ROWS, 128), 1)

    def copy_of(j, owner, rank):
        rows = pl.ds(pl.multiple_of(rank * GROUPS * BLK, GROUPS * BLK), GROUPS * BLK)
        return pltpu.make_async_copy(staged.at[j], parts.at[owner, rows], sems.at[j])

    def send(j, _):
        owner = lax.shift_right_logical(dest[j], 5)
        rank = count[owner]
        count[owner] = rank + 1
        rows = pl.ds(pl.multiple_of(j * BLK, BLK), BLK)
        for g in range(GROUPS):
            staged[j, g * BLK : (g + 1) * BLK] = packed[rows, g * 128 : (g + 1) * 128]
        copy_of(j, owner, rank).start()
        label = (dest[j] & (NSEQ - 1)) + 1
        new = jnp.where(lane == rank, label.astype(F32), labels[owner].astype(F32))
        labels[owner] = new.astype(BF16)
        return 0

    per = BLK // LOADS
    for i in range(LOADS):
        loads[i].wait()
        lax.fori_loop(i * per, (i + 1) * per, send, 0)
    last = pltpu.make_async_copy(labels, parts.at[:, pl.ds(PIECES, LABEL_ROWS)], label_sem)
    last.start()

    def finish(j, _):
        copy_of(j, 0, 0).wait()
        return 0

    lax.fori_loop(0, BLK, finish, 0)
    last.wait()


def pack(packed, dest):
    return pl.pallas_call(
        pack_kernel,
        out_shape=jax.ShapeDtypeStruct((NSEQ, PIECES + LABEL_ROWS, 128), BF16),
        in_specs=[SMEM, ANY],
        out_specs=ANY,
        scratch_shapes=[
            pltpu.VMEM((SDEV, D), BF16),
            pltpu.VMEM((BLK, GROUPS * BLK, 128), BF16),
            pltpu.VMEM((NSEQ, LABEL_ROWS, 128), BF16),
            pltpu.SMEM((NSEQ,), jnp.int32),
            dma(LOADS),
            dma(BLK),
            dma(),
        ],
        compiler_params=pltpu.CompilerParams(vmem_limit_bytes=PACK_VMEM),
        name="pack_blocks",
    )(dest, packed)


def project_kernel(
    received_h, w_qkv_h, b_qkv,
    x, q, kv, head, tail,
    received, marks, w_qkv, vector, labels, sem, rsem, wsem,
):
    mark = pltpu.make_async_copy(received_h.at[:, pl.ds(PIECES, LABEL_ROWS)], marks, sem)
    mark.start()
    step = NSEQ // LOADS
    parts = [
        pltpu.make_async_copy(
            received_h.at[pl.ds(i * step, step), pl.ds(0, PIECES)],
            received.at[pl.ds(i * step, step)],
            rsem.at[i],
        )
        for i in range(LOADS)
    ]
    start_all(parts)
    columns = [pl.ds(D, D), pl.ds(2 * D, D), pl.ds(0, D)]
    loads = [
        pltpu.make_async_copy(w_qkv_h.at[:, c], w_qkv.at[:, c], wsem.at[i])
        for i, c in enumerate(columns)
    ]
    start_all(loads)
    mark.wait()
    vector[...] = jnp.max(marks[...].astype(F32), axis=1).astype(jnp.int32)
    copy = pltpu.make_async_copy(vector, labels, sem)
    copy.start()
    copy.wait()

    def fetch(source, _):
        for rank in range(CAP):
            label = labels[source, rank]

            @pl.when(label > 0)
            def _():
                rows = pl.ds(pl.multiple_of((label - 1) * BLK, BLK), BLK)
                for g in range(GROUPS):
                    x[rows, g * 128 : (g + 1) * 128] = received[source, piece(rank, g)]

        return 0

    for i in range(LOADS):
        parts[i].wait()
        lax.fori_loop(i * step, (i + 1) * step, fetch, 0)
    for i in range(2):
        loads[i].wait()
        part = dot(x[...], w_qkv[:, columns[i]]) + b_qkv[:, columns[i]]
        kv[:, pl.ds(i * D, D)] = part.astype(BF16)
        head[:, pl.ds(i * D, D)] = part[:BAND].astype(BF16)
        tail[:, pl.ds(i * D, D)] = part[SDEV - BAND :].astype(BF16)
    loads[2].wait()
    q[...] = ((dot(x[...], w_qkv[:, :D]) + b_qkv[:, :D]) * (LOG2E / 8.0)).astype(BF16)


def project(received, w_qkv, b_qkv):
    shapes = [(SDEV, D), (SDEV, D), (SDEV, 2 * D), (BAND, 2 * D), (BAND, 2 * D)]
    return pl.pallas_call(
        project_kernel,
        out_shape=[jax.ShapeDtypeStruct(shape, BF16) for shape in shapes],
        in_specs=[ANY, ANY, VMEM],
        out_specs=[VMEM] * 5,
        scratch_shapes=[
            pltpu.VMEM((NSEQ, PIECES, 128), BF16),
            pltpu.VMEM((NSEQ, LABEL_ROWS, 128), BF16),
            pltpu.VMEM((D, 3 * D), BF16),
            pltpu.VMEM((NSEQ, 128), jnp.int32),
            pltpu.SMEM((NSEQ, 128), jnp.int32),
            dma(),
            dma(LOADS),
            dma(3),
        ],
        compiler_params=pltpu.CompilerParams(vmem_limit_bytes=PROJECT_VMEM),
        name="project_tokens",
    )(received, w_qkv, b_qkv)


def doc_bounds(info, doc_len, start):
    u0 = info[0] + LEAD + start
    doc = lax.shift_right_logical(u0, 13)
    base = doc * DOC_LEN
    length = doc_len[doc]
    low = jnp.maximum(0, LEAD - base)
    high = jnp.minimum(length, SPAN + LEAD - base)
    return u0 - base, length, low, high


def reach_table(info, doc_len, start):
    rel, _, low, high = doc_bounds(info, doc_len, start)
    j = iota((CH, WIN), 1)
    dist = jnp.abs(iota((CH, WIN), 0) + BAND - j)
    key = rel - BAND + j
    keep = (dist <= BAND) & (((key >= low) & (key < high)) | (dist == 0))
    return jnp.where(keep, -dist.astype(F32), FAR)


def layer_norm(v, gain, shift):
    centre = jnp.mean(v, axis=-1, keepdims=True)
    v = v - centre
    spread = jnp.mean(v * v, axis=-1, keepdims=True)
    return v * lax.rsqrt(spread + norm_eps) * gain + shift


def gelu(x):
    z = jnp.abs(x)
    t = 1.0 / (1.0 + z * (0.3275911 * math.sqrt(0.5)))
    p = t * (0.5 * 1.061405429) + (0.5 * -1.453152027)
    p = p * t + (0.5 * 1.421413741)
    p = p * t + (0.5 * -0.284496736)
    p = p * t + (0.5 * 0.254829592)
    q = p * t * jnp.exp2(x * x * (-0.5 * LOG2E))
    return jnp.maximum(x, 0.0) - z * q


def attend_pair(pair, chunks, q, window, reach, slopes, att):
    lanes = pl.ds(pair * 128, 128)
    vlanes = pl.ds(D + pair * 128, 128)
    left = iota((CH, 128), 1) < 64
    ones = jnp.ones((WIN, 128), BF16)
    outside = jnp.zeros((HALF, WIN - KEYS), BF16)
    for n, c in enumerate(chunks):
        mine = q[pl.ds(c * CH, CH), lanes]
        none = jnp.zeros_like(mine)
        both = jnp.concatenate([jnp.where(left, mine, none), jnp.where(left, none, mine)], axis=0)
        scores = lax.dot_general(
            both, window(c, lanes), (((1,), (1,)), ((), ())), preferred_element_type=F32
        )
        probs = []
        for side in range(2):
            for half in range(2):
                row = half * HALF
                keys = slice(half * HALF, half * HALF + KEYS)
                s = scores[side * CH + row : side * CH + row + HALF, keys]
                s = s + slopes[2 * pair + side] * reach[n, row : row + HALF, keys]
                p = jnp.exp2(s - jnp.max(s, axis=-1, keepdims=True)).astype(BF16)
                probs.append(jnp.concatenate([outside, p] if half else [p, outside], axis=1))
        v = jnp.concatenate([window(c, vlanes), ones], axis=1)
        o = dot(jnp.concatenate(probs, axis=0), v)
        o = o[:, :128] / o[:, 128:]
        att[pl.ds(n * CH, CH), lanes] = jnp.where(left, o[:CH], o[CH:]).astype(BF16)


def pool_tile(info, doc_len, lists, chunk, enc, centroids):
    rel, length, _, _ = doc_bounds(info, doc_len, chunk * CH)
    r = iota((TROWS, CH), 0)
    i = iota((TROWS, CH), 1)
    scale = jnp.where(length - rel - 2 * r >= 2, 0.5, 1.0)
    mine = (lax.shift_right_logical(i, 1) == r) & (rel + i < length)
    pooled = dot(jnp.where(mine, scale, 0.0).astype(BF16), enc)
    pick = (iota((TROWS, centroids.shape[0]), 1) == lists[chunk]).astype(BF16)
    return (pooled - dot(pick, centroids[...])).astype(BF16)


def start_all(copies):
    for c in copies:
        c.start()


def wait_all(copies):
    for c in copies:
        c.wait()


def layer_of(att, x, start, first, active, enc, ws, loads, vecs):
    w_out, w_glu, w_down = ws
    b_out, g1, s1, b_down, g2, s2 = vecs
    count = att.shape[0]
    part = count // 2
    loads[0].wait()
    for r in range(0, count, part):
        rows = pl.ds(r, part)
        mixed = dot(att[rows], w_out[...]) + b_out[...] + x[pl.ds(start + r, part)].astype(F32)
        first[rows] = layer_norm(mixed, g1[...], s1[...]).astype(BF16)
    loads[1].wait()
    for i in range(FF // FC):
        cols = pl.ds(i * FC, FC)
        up = pl.ds(FF + i * FC, FC)
        f = first[...]
        active[:, cols] = (gelu(dot(f, w_glu[:, cols])) * dot(f, w_glu[:, up])).astype(BF16)
    loads[2].wait()
    for r in range(0, count, part):
        rows = pl.ds(r, part)
        second = dot(active[rows], w_down[...]) + b_down[...] + first[rows].astype(F32)
        enc[rows] = layer_norm(second, g2[...], s2[...]).astype(BF16)


def loads_of(sources, targets, sems):
    return [pltpu.make_async_copy(s, t, sems.at[i]) for i, (s, t) in enumerate(zip(sources, targets))]


def layer_kernel(
    chunks, before, info, doc_len, lists, slopes,
    enc_in, w_out_h, w_glu_h, w_down_h, x, q, kv, *rest,
):
    halo = None if before is None else rest[0]
    b_out, g1, s1, b_down, g2, s2, centroids = rest[:7] if halo is None else rest[1:8]
    enc_h, *tiles, w_out, w_glu, w_down, att, first, active, reach, enc, wsem, osem = rest[
        {None: 7, True: 9, False: 8}[before] :
    ]
    ws = (w_out, w_glu, w_down)
    loads = loads_of((w_out_h, w_glu_h, w_down_h), ws, wsem)
    start_all(loads)
    start = chunks[0] * CH
    rows = len(chunks) * CH
    for n, c in enumerate(chunks):
        reach[n] = reach_table(info, doc_len, c * CH)

    def window(c, lanes):
        if halo is None:
            return kv[pl.ds(c * CH - BAND, WIN), lanes]
        own = kv[pl.ds(0 if before else c * CH - BAND, WIN - BAND), lanes]
        return jnp.concatenate([halo[:, lanes], own] if before else [own, halo[:, lanes]], axis=0)

    for pair in range(H // 2):
        attend_pair(pair, chunks, q, window, reach, slopes, att)
    layer_of(att, x, start, first, active, enc, ws, loads, (b_out, g1, s1, b_down, g2, s2))
    last = pltpu.make_async_copy(enc, enc_h.at[pl.ds(start, rows)], osem)
    last.start()
    for n, c in enumerate(chunks):
        tile = pool_tile(info, doc_len, lists, c, enc[pl.ds(n * CH, CH)], centroids)
        if before:
            att[pl.ds(0, TROWS)] = tile
            send_tiles(info, lists, att.at[pl.ds(0, TROWS)], rest[8], tiles)
        else:
            tiles[0][n] = tile
    last.wait()


def send_tiles(info, lists, tile_0, tiles_12, groups):
    owners = [lax.shift_right_logical(lists[t], 6) for t in range(3)]
    for g in groups:
        g[...] = jnp.zeros_like(g)
    for t in range(3):
        rank = sum([(owners[e] == owners[t]).astype(jnp.int32) for e in range(t)], jnp.int32(0))
        turn = (owners[t] + BATCHES - info[1]) & (BATCHES - 1)
        for k, g in enumerate(groups):

            @pl.when(turn == k)
            def _():
                g[rank] = tile_0[...] if t == 0 else tiles_12[t - 1]


def dma(*shape):
    return pltpu.SemaphoreType.DMA(shape)


def layer(chunks, scalars, enc, ws, x, q, kv, vecs, halo=None, before=None, tiles_12=None):
    rows = len(chunks) * CH
    rest = (x, q, kv) + (() if halo is None else (halo,)) + vecs
    rest += () if tiles_12 is None else (tiles_12,)
    tiles = [(CAP, TROWS, D)] * BATCHES if before else [(len(chunks), TROWS, D)]
    return pl.pallas_call(
        functools.partial(layer_kernel, chunks, before),
        out_shape=(
            jax.ShapeDtypeStruct((SDEV, D), BF16),
            *[jax.ShapeDtypeStruct(shape, BF16) for shape in tiles],
        ),
        in_specs=[SMEM] * 4 + [ANY] * 4 + [VMEM] * len(rest),
        out_specs=(ANY,) + (VMEM,) * len(tiles),
        input_output_aliases={} if halo is None else {4: 0},
        scratch_shapes=[
            pltpu.VMEM((D, D), BF16),
            pltpu.VMEM((D, 2 * FF), BF16),
            pltpu.VMEM((FF, D), BF16),
            pltpu.VMEM((rows, D), BF16),
            pltpu.VMEM((rows, D), BF16),
            pltpu.VMEM((rows, FF), BF16),
            pltpu.VMEM((len(chunks), CH, WIN), F32),
            pltpu.VMEM((rows, D), BF16),
            dma(3),
            dma(),
        ],
        compiler_params=pltpu.CompilerParams(vmem_limit_bytes=KERNEL_VMEM),
        cost_estimate=pl.CostEstimate(
            flops=12_000_000 * rows, bytes_accessed=20_000_000, transcendentals=16_000 * rows
        ),
        name="layer_chunk_%d" % chunks[0],
    )(*scalars, enc, *ws, *rest)


def store_kernel(info, *refs):
    groups, out, sems = refs[:BATCHES], refs[BATCHES], refs[BATCHES + 1]
    moves = []
    for k in range(BATCHES):
        device = (info[1] + BATCHES - k) & (BATCHES - 1)
        for r in range(CAP):
            row = pl.multiple_of((device * CAP + r) * TROWS, TROWS)
            dst = out.at[pl.ds(row, TROWS)]
            moves.append(pltpu.make_async_copy(groups[k].at[r], dst, sems.at[k * CAP + r]))
    start_all(moves)
    wait_all(moves)


def store(info, groups):
    return pl.pallas_call(
        store_kernel,
        out_shape=jax.ShapeDtypeStruct((BATCHES * CAP * TROWS, D), BF16),
        in_specs=[SMEM] + [VMEM] * BATCHES,
        out_specs=ANY,
        scratch_shapes=[dma(BATCHES * CAP)],
        compiler_params=pltpu.CompilerParams(vmem_limit_bytes=SMALL_VMEM),
        name="store_tiles",
    )(info, *groups)


def store_last_kernel(info, lists, *refs):
    singles, out, sems = refs[:BATCHES], refs[BATCHES + 1], refs[BATCHES + 2]
    moves = []
    for k in range(BATCHES):
        device = (info[1] + BATCHES - k) & (BATCHES - 1)
        mine = [lax.shift_right_logical(lists[k * 4 + t], 6) == info[1] for t in range(4)]
        rank = sum([m.astype(jnp.int32) for m in mine[:3]], jnp.int32(0))
        row = pl.multiple_of((device * CAP + jnp.minimum(rank, CAP - 1)) * TROWS, TROWS)
        dst = out.at[pl.ds(row, TROWS)]
        moves.append((mine[3], pltpu.make_async_copy(singles[k].at[0], dst, sems.at[k])))
    for go, copy in moves:
        pl.when(go)(copy.start)
    for go, copy in moves:
        pl.when(go)(copy.wait)


def store_last(info, lists, singles, stored):
    return pl.pallas_call(
        store_last_kernel,
        out_shape=jax.ShapeDtypeStruct(stored.shape, BF16),
        in_specs=[SMEM] * 2 + [VMEM] * BATCHES + [ANY],
        out_specs=ANY,
        input_output_aliases={2 + BATCHES: 0},
        scratch_shapes=[dma(BATCHES)],
        compiler_params=pltpu.CompilerParams(vmem_limit_bytes=SMALL_VMEM),
        name="store_last_tile",
    )(info, lists, *singles, stored)


def on_device(
    packed, block_dest, doc_len, w_qkv, b_qkv, w_out, b_out, norm1_gain, norm1_shift,
    w_glu, w_down, b_down, norm2_gain, norm2_shift, centroids, tile_list,
):
    seq_here = lax.axis_index("seq")
    batch_here = lax.axis_index("batch")

    def from_batch(values):
        far = {}
        for k in (1, 3, 2):
            turn = [(i, (i + k) % BATCHES) for i in range(BATCHES)]
            far[k] = lax.ppermute(values[k], "batch", turn)
        return [values[0], far[1], far[2], far[3]]

    received = lax.all_to_all(
        pack(packed, block_dest), "seq", split_axis=0, concat_axis=0, tiled=True
    )
    lists = jnp.concatenate(from_batch([tile_list] * BATCHES))
    info = jnp.stack([seq_here * SDEV, batch_here]).astype(jnp.int32)
    slopes = jnp.asarray(head_slopes(H) * np.float32(LOG2E))
    row = lambda v: v.reshape(1, -1)
    ws = (w_out, w_glu, w_down)
    vecs = (
        row(b_out), row(norm1_gain), row(norm1_shift),
        row(b_down), row(norm2_gain), row(norm2_shift), centroids,
    )
    x, q, kv, head, tail = project(received, w_qkv, row(b_qkv))
    up = [(i, i + 1) for i in range(NSEQ - 1)]
    down = [(j, i) for i, j in up]
    before = lax.ppermute(tail, "seq", up)
    after = lax.ppermute(head, "seq", down)
    scalars = (info, doc_len, lists, slopes)
    enc, tiles_12 = layer((1, 2), scalars, x, ws, x, q, kv, vecs)
    enc, *groups = layer(
        (0,), scalars, enc, ws, x, q, kv, vecs, halo=before, before=True, tiles_12=tiles_12
    )
    groups = from_batch(groups)
    enc, tile_3 = layer((3,), scalars, enc, ws, x, q, kv, vecs, halo=after, before=False)
    lasts = from_batch([tile_3] * BATCHES)
    stored = store_last(info, lists, lasts, store(info, groups))
    return enc, stored.reshape(1, 1, BATCHES * CAP * TROWS, D)


def solution(mesh):
    return jax.shard_map(
        on_device,
        mesh=mesh,
        in_specs=(
            P(("batch", "seq"), None),
            P(("batch", "seq")),
            P("batch"),
            P(), P(), P(), P(), P(), P(), P(), P(), P(), P(), P(), P(),
            P(("batch", "seq")),
        ),
        out_specs=(P(("batch", "seq"), None), P("batch", "seq", None, None)),
        check_vma=False,
    )
```

```python
import functools
import math

import jax
import jax.numpy as jnp
import numpy as np
from jax import lax
from jax.experimental import pallas as pl
from jax.experimental.pallas import tpu as pltpu
from jax.sharding import PartitionSpec as P

H = 12
D = 768
FF = 3072
DOC_LEN = 8192
BAND = 256
CAP = 2
TROWS = 128
LPO = 64
NSEQ = 32
BATCHES = 4
SDEV = 1024
BLK = 32
LEAD = 512
SPAN = NSEQ * SDEV
CH = 256
WIN = CH + 2 * BAND
HALF = CH // 2
KEYS = HALF + 2 * BAND
GROUPS = D // 128
PIECES = CAP * GROUPS * BLK
LABEL_ROWS = 16
LOADS = 4
FC = 768

norm_eps = 1e-06
LOG2E = math.log2(math.e)
FAR = -1e32
MIB = 1 << 20
KERNEL_VMEM = 42 * MIB
SMALL_VMEM = 8 * MIB
TINY_VMEM = MIB
PACK_VMEM = 56 * MIB
PROJECT_VMEM = 30 * MIB

ANY = pl.BlockSpec(memory_space=pl.ANY)
VMEM = pl.BlockSpec(memory_space=pltpu.VMEM)
SMEM = pl.BlockSpec(memory_space=pltpu.SMEM)
F32 = jnp.float32
BF16 = jnp.bfloat16


def head_slopes(heads):
    base = 2 ** int(np.floor(np.log2(heads)))
    first = [2.0 ** (-8.0 * (i + 1) / base) for i in range(base)]
    extra = [2.0 ** (-4.0 * (i + 1) / base) for i in range(2 * (heads - base))][0::2]
    return np.asarray(first + extra, np.float32)


def iota(shape, dim):
    return lax.broadcasted_iota(jnp.int32, shape, dim)


def dot(a, b):
    return jnp.dot(a, b, preferred_element_type=F32)


def piece(rank, group):
    return pl.ds(pl.multiple_of((rank * GROUPS + group) * BLK, BLK), BLK)


def pack_kernel(dest, packed_h, parts, packed, staged, labels, count, load_sems, sems, label_sem):
    step = SDEV // LOADS
    loads = [
        pltpu.make_async_copy(
            packed_h.at[pl.ds(i * step, step)], packed.at[pl.ds(i * step, step)], load_sems.at[i]
        )
        for i in range(LOADS)
    ]
    start_all(loads)
    labels[...] = jnp.zeros_like(labels)

    for i in range(NSEQ):
        count[i] = 0
    lane = iota((LABEL_ROWS, 128), 1)

    def copy_of(j, owner, rank):
        rows = pl.ds(pl.multiple_of(rank * GROUPS * BLK, GROUPS * BLK), GROUPS * BLK)
        return pltpu.make_async_copy(staged.at[j], parts.at[owner, rows], sems.at[j])

    def send(j, _):
        owner = lax.shift_right_logical(dest[j], 5)
        rank = count[owner]
        count[owner] = rank + 1
        rows = pl.ds(pl.multiple_of(j * BLK, BLK), BLK)
        for g in range(GROUPS):
            staged[j, g * BLK : (g + 1) * BLK] = packed[rows, g * 128 : (g + 1) * 128]
        copy_of(j, owner, rank).start()
        label = (dest[j] & (NSEQ - 1)) + 1
        new = jnp.where(lane == rank, label.astype(F32), labels[owner].astype(F32))
        labels[owner] = new.astype(BF16)
        return 0

    per = BLK // LOADS
    for i in range(LOADS):
        loads[i].wait()
        lax.fori_loop(i * per, (i + 1) * per, send, 0, unroll=True)
    last = pltpu.make_async_copy(labels, parts.at[:, pl.ds(PIECES, LABEL_ROWS)], label_sem)
    last.start()

    for j in range(BLK):
        copy_of(j, 0, 0).wait()
    last.wait()


def pack(packed, dest):
    return pl.pallas_call(
        pack_kernel,
        out_shape=jax.ShapeDtypeStruct((NSEQ, PIECES + LABEL_ROWS, 128), BF16),
        in_specs=[SMEM, ANY],
        out_specs=ANY,
        scratch_shapes=[
            pltpu.VMEM((SDEV, D), BF16),
            pltpu.VMEM((BLK, GROUPS * BLK, 128), BF16),
            pltpu.VMEM((NSEQ, LABEL_ROWS, 128), BF16),
            pltpu.SMEM((NSEQ,), jnp.int32),
            dma(LOADS),
            dma(BLK),
            dma(),
        ],
        compiler_params=pltpu.CompilerParams(vmem_limit_bytes=PACK_VMEM),
        name="pack_blocks",
    )(dest, packed)


def project_kernel(
    received_h, w_qkv, b_qkv,
    x, q, kv, head, tail,
    received, marks, vector, labels, where, sem, rsem,
):
    mark = pltpu.make_async_copy(received_h.at[:, pl.ds(PIECES, LABEL_ROWS)], marks, sem)
    mark.start()
    step = NSEQ // LOADS
    parts = [
        pltpu.make_async_copy(
            received_h.at[pl.ds(i * step, step), pl.ds(0, PIECES)],
            received.at[pl.ds(i * step, step)],
            rsem.at[i],
        )
        for i in range(LOADS)
    ]
    start_all(parts)
    mark.wait()
    vector[...] = jnp.max(marks[...].astype(F32), axis=1).astype(jnp.int32)
    copy = pltpu.make_async_copy(vector, labels, sem)
    copy.start()
    copy.wait()

    for source in range(NSEQ):
        for rank in range(CAP):
            where[labels[source, rank]] = source * CAP + rank
    wait_all(parts)

    def fetch(place, _):
        slot = where[1 + place]
        source = lax.shift_right_logical(slot, 1)
        rows = pl.ds(pl.multiple_of(place * BLK, BLK), BLK)
        for g in range(GROUPS):
            x[rows, g * 128 : (g + 1) * 128] = received[source, piece(slot & 1, g)]
        return 0

    lax.fori_loop(0, SDEV // BLK, fetch, 0, unroll=8)
    for i in range(2):
        columns = pl.ds((i + 1) * D, D)
        part = dot(x[...], w_qkv[:, columns]) + b_qkv[:, columns]
        kv[:, pl.ds(i * D, D)] = part.astype(BF16)
        head[:, pl.ds(i * D, D)] = part[:BAND].astype(BF16)
        tail[:, pl.ds(i * D, D)] = part[SDEV - BAND :].astype(BF16)
    q[...] = ((dot(x[...], w_qkv[:, :D]) + b_qkv[:, :D]) * (LOG2E / 8.0)).astype(BF16)


def project(received, w_qkv, b_qkv):
    shapes = [(SDEV, D), (SDEV, D), (SDEV, 2 * D), (BAND, 2 * D), (BAND, 2 * D)]
    return pl.pallas_call(
        project_kernel,
        out_shape=[jax.ShapeDtypeStruct(shape, BF16) for shape in shapes],
        in_specs=[ANY, VMEM, VMEM],
        out_specs=[VMEM] * 5,
        scratch_shapes=[
            pltpu.VMEM((NSEQ, PIECES, 128), BF16),
            pltpu.VMEM((NSEQ, LABEL_ROWS, 128), BF16),
            pltpu.VMEM((NSEQ, 128), jnp.int32),
            pltpu.SMEM((NSEQ, 128), jnp.int32),
            pltpu.SMEM((SDEV // BLK + 1,), jnp.int32),
            dma(),
            dma(LOADS),
        ],
        compiler_params=pltpu.CompilerParams(vmem_limit_bytes=PROJECT_VMEM),
        name="project_tokens",
    )(received, w_qkv, b_qkv)


def load_kernel(source, target, sem):
    copy = pltpu.make_async_copy(source, target, sem)
    copy.start()
    copy.wait()


def load(w):
    return pl.pallas_call(
        load_kernel,
        out_shape=jax.ShapeDtypeStruct(w.shape, w.dtype),
        in_specs=[ANY],
        out_specs=VMEM,
        scratch_shapes=[dma()],
        compiler_params=pltpu.CompilerParams(vmem_limit_bytes=TINY_VMEM),
        cost_estimate=pl.CostEstimate(flops=0, bytes_accessed=2 * w.size, transcendentals=0),
        name="load_weights",
    )(w)


def doc_bounds(info, doc_len, start):
    u0 = info[0] + LEAD + start
    doc = lax.shift_right_logical(u0, 13)
    base = doc * DOC_LEN
    length = doc_len[doc]
    low = jnp.maximum(0, LEAD - base)
    high = jnp.minimum(length, SPAN + LEAD - base)
    return u0 - base, length, low, high


def reach_table(info, doc_len, start):
    rel, _, low, high = doc_bounds(info, doc_len, start)
    j = iota((CH, WIN), 1)
    dist = jnp.abs(iota((CH, WIN), 0) + BAND - j)
    key = rel - BAND + j
    keep = (dist <= BAND) & (((key >= low) & (key < high)) | (dist == 0))
    return jnp.where(keep, -dist.astype(F32), FAR)


def layer_norm(v, gain, shift):
    centre = jnp.mean(v, axis=-1, keepdims=True)
    v = v - centre
    spread = jnp.mean(v * v, axis=-1, keepdims=True)
    return v * lax.rsqrt(spread + norm_eps) * gain + shift


def gelu(x):
    z = jnp.abs(x)
    t = 1.0 / (1.0 + z * (0.3275911 * math.sqrt(0.5)))
    p = t * (0.5 * 1.061405429) + (0.5 * -1.453152027)
    p = p * t + (0.5 * 1.421413741)
    p = p * t + (0.5 * -0.284496736)
    p = p * t + (0.5 * 0.254829592)
    q = p * t * jnp.exp2(x * x * (-0.5 * LOG2E))
    return jnp.maximum(x, 0.0) - z * q


def attend_pair(pair, chunks, q, window, reach, slopes, att):
    lanes = pl.ds(pair * 128, 128)
    vlanes = pl.ds(D + pair * 128, 128)
    left = iota((CH, 128), 1) < 64
    ones = jnp.ones((WIN, 128), BF16)
    outside = jnp.zeros((HALF, WIN - KEYS), BF16)
    for n, c in enumerate(chunks):
        mine = q[pl.ds(c * CH, CH), lanes]
        none = jnp.zeros_like(mine)
        both = jnp.concatenate([jnp.where(left, mine, none), jnp.where(left, none, mine)], axis=0)
        scores = lax.dot_general(
            both, window(c, lanes), (((1,), (1,)), ((), ())), preferred_element_type=F32
        )
        probs = []
        for side in range(2):
            for half in range(2):
                row = half * HALF
                keys = slice(half * HALF, half * HALF + KEYS)
                s = scores[side * CH + row : side * CH + row + HALF, keys]
                s = s + slopes[2 * pair + side] * reach[n, row : row + HALF, keys]
                p = jnp.exp2(s - jnp.max(s, axis=-1, keepdims=True)).astype(BF16)
                probs.append(jnp.concatenate([outside, p] if half else [p, outside], axis=1))
        v = jnp.concatenate([window(c, vlanes), ones], axis=1)
        o = dot(jnp.concatenate(probs, axis=0), v)
        o = o[:, :128] / o[:, 128:]
        att[pl.ds(n * CH, CH), lanes] = jnp.where(left, o[:CH], o[CH:]).astype(BF16)


def pool_tile(info, doc_len, lists, chunk, enc, centroids):
    rel, length, _, _ = doc_bounds(info, doc_len, chunk * CH)
    r = iota((TROWS, CH), 0)
    i = iota((TROWS, CH), 1)
    scale = jnp.where(length - rel - 2 * r >= 2, 0.5, 1.0)
    mine = (lax.shift_right_logical(i, 1) == r) & (rel + i < length)
    pooled = dot(jnp.where(mine, scale, 0.0).astype(BF16), enc)
    pick = (iota((TROWS, centroids.shape[0]), 1) == lists[chunk]).astype(BF16)
    return (pooled - dot(pick, centroids[...])).astype(BF16)


def start_all(copies):
    for c in copies:
        c.start()


def wait_all(copies):
    for c in copies:
        c.wait()


def layer_of(att, x, start, first, active, enc, ws, loads, vecs):
    w_out, w_glu, w_down = ws
    b_out, g1, s1, b_down, g2, s2 = vecs
    count = att.shape[0]
    part = count // 2
    loads[0].wait()
    for r in range(0, count, part):
        rows = pl.ds(r, part)
        mixed = dot(att[rows], w_out[...]) + b_out[...] + x[pl.ds(start + r, part)].astype(F32)
        first[rows] = layer_norm(mixed, g1[...], s1[...]).astype(BF16)
    loads[1].wait()
    for i in range(FF // FC):
        cols = pl.ds(i * FC, FC)
        up = pl.ds(FF + i * FC, FC)
        f = first[...]
        active[:, cols] = (gelu(dot(f, w_glu[:, cols])) * dot(f, w_glu[:, up])).astype(BF16)
    loads[2].wait()
    for r in range(0, count, part):
        rows = pl.ds(r, part)
        second = dot(active[rows], w_down[...]) + b_down[...] + first[rows].astype(F32)
        enc[rows] = layer_norm(second, g2[...], s2[...]).astype(BF16)


def loads_of(sources, targets, sems):
    return [pltpu.make_async_copy(s, t, sems.at[i]) for i, (s, t) in enumerate(zip(sources, targets))]


def layer_kernel(
    chunks, before, info, doc_len, lists, slopes,
    enc_in, w_out_h, w_glu_h, w_down_h, x, q, kv, *rest,
):
    halo = None if before is None else rest[0]
    b_out, g1, s1, b_down, g2, s2, centroids = rest[:7] if halo is None else rest[1:8]
    enc_h, *tiles, w_out, w_glu, w_down, att, first, active, reach, enc, wsem, osem = rest[
        {None: 7, True: 9, False: 8}[before] :
    ]
    ws = (w_out, w_glu, w_down)
    loads = loads_of((w_out_h, w_glu_h, w_down_h), ws, wsem)
    start_all(loads)
    start = chunks[0] * CH
    rows = len(chunks) * CH
    for n, c in enumerate(chunks):
        reach[n] = reach_table(info, doc_len, c * CH)

    def window(c, lanes):
        if halo is None:
            return kv[pl.ds(c * CH - BAND, WIN), lanes]
        own = kv[pl.ds(0 if before else c * CH - BAND, WIN - BAND), lanes]
        return jnp.concatenate([halo[:, lanes], own] if before else [own, halo[:, lanes]], axis=0)

    for pair in range(H // 2):
        attend_pair(pair, chunks, q, window, reach, slopes, att)
    layer_of(att, x, start, first, active, enc, ws, loads, (b_out, g1, s1, b_down, g2, s2))
    last = pltpu.make_async_copy(enc, enc_h.at[pl.ds(start, rows)], osem)
    last.start()
    for n, c in enumerate(chunks):
        tile = pool_tile(info, doc_len, lists, c, enc[pl.ds(n * CH, CH)], centroids)
        if before:
            att[pl.ds(0, TROWS)] = tile
            send_tiles(info, lists, att.at[pl.ds(0, TROWS)], rest[8], tiles)
        else:
            tiles[0][n] = tile
    last.wait()


def send_tiles(info, lists, tile_0, tiles_12, groups):
    owners = [lax.shift_right_logical(lists[t], 6) for t in range(3)]
    for g in groups:
        g[...] = jnp.zeros_like(g)
    for t in range(3):
        rank = sum([(owners[e] == owners[t]).astype(jnp.int32) for e in range(t)], jnp.int32(0))
        turn = (owners[t] + BATCHES - info[1]) & (BATCHES - 1)
        for k, g in enumerate(groups):

            @pl.when(turn == k)
            def _():
                g[rank] = tile_0[...] if t == 0 else tiles_12[t - 1]


def dma(*shape):
    return pltpu.SemaphoreType.DMA(shape)


def layer(chunks, scalars, enc, ws, x, q, kv, vecs, halo=None, before=None, tiles_12=None):
    rows = len(chunks) * CH
    rest = (x, q, kv) + (() if halo is None else (halo,)) + vecs
    rest += () if tiles_12 is None else (tiles_12,)
    tiles = [(CAP, TROWS, D)] * BATCHES if before else [(len(chunks), TROWS, D)]
    return pl.pallas_call(
        functools.partial(layer_kernel, chunks, before),
        out_shape=(
            jax.ShapeDtypeStruct((SDEV, D), BF16),
            *[jax.ShapeDtypeStruct(shape, BF16) for shape in tiles],
        ),
        in_specs=[SMEM] * 4 + [ANY] * 4 + [VMEM] * len(rest),
        out_specs=(ANY,) + (VMEM,) * len(tiles),
        input_output_aliases={} if halo is None else {4: 0},
        scratch_shapes=[
            pltpu.VMEM((D, D), BF16),
            pltpu.VMEM((D, 2 * FF), BF16),
            pltpu.VMEM((FF, D), BF16),
            pltpu.VMEM((rows, D), BF16),
            pltpu.VMEM((rows, D), BF16),
            pltpu.VMEM((rows, FF), BF16),
            pltpu.VMEM((len(chunks), CH, WIN), F32),
            pltpu.VMEM((rows, D), BF16),
            dma(3),
            dma(),
        ],
        compiler_params=pltpu.CompilerParams(vmem_limit_bytes=KERNEL_VMEM),
        cost_estimate=pl.CostEstimate(
            flops=12_000_000 * rows, bytes_accessed=20_000_000, transcendentals=16_000 * rows
        ),
        name="layer_chunk_%d" % chunks[0],
    )(*scalars, enc, *ws, *rest)


def store_kernel(info, *refs):
    groups, out, sems = refs[:BATCHES], refs[BATCHES], refs[BATCHES + 1]
    moves = []
    for k in range(BATCHES):
        device = (info[1] + BATCHES - k) & (BATCHES - 1)
        for r in range(CAP):
            row = pl.multiple_of((device * CAP + r) * TROWS, TROWS)
            dst = out.at[pl.ds(row, TROWS)]
            moves.append(pltpu.make_async_copy(groups[k].at[r], dst, sems.at[k * CAP + r]))
    start_all(moves)
    wait_all(moves)


def store(info, groups):
    return pl.pallas_call(
        store_kernel,
        out_shape=jax.ShapeDtypeStruct((BATCHES * CAP * TROWS, D), BF16),
        in_specs=[SMEM] + [VMEM] * BATCHES,
        out_specs=ANY,
        scratch_shapes=[dma(BATCHES * CAP)],
        compiler_params=pltpu.CompilerParams(vmem_limit_bytes=SMALL_VMEM),
        name="store_tiles",
    )(info, *groups)


def store_last_kernel(info, lists, *refs):
    singles, out, sems = refs[:BATCHES], refs[BATCHES + 1], refs[BATCHES + 2]
    moves = []
    for k in range(BATCHES):
        device = (info[1] + BATCHES - k) & (BATCHES - 1)
        mine = [lax.shift_right_logical(lists[k * 4 + t], 6) == info[1] for t in range(4)]
        rank = sum([m.astype(jnp.int32) for m in mine[:3]], jnp.int32(0))
        row = pl.multiple_of((device * CAP + jnp.minimum(rank, CAP - 1)) * TROWS, TROWS)
        dst = out.at[pl.ds(row, TROWS)]
        moves.append((mine[3], pltpu.make_async_copy(singles[k].at[0], dst, sems.at[k])))
    for go, copy in moves:
        pl.when(go)(copy.start)
    for go, copy in moves:
        pl.when(go)(copy.wait)


def store_last(info, lists, singles, stored):
    return pl.pallas_call(
        store_last_kernel,
        out_shape=jax.ShapeDtypeStruct(stored.shape, BF16),
        in_specs=[SMEM] * 2 + [VMEM] * BATCHES + [ANY],
        out_specs=ANY,
        input_output_aliases={2 + BATCHES: 0},
        scratch_shapes=[dma(BATCHES)],
        compiler_params=pltpu.CompilerParams(vmem_limit_bytes=SMALL_VMEM),
        name="store_last_tile",
    )(info, lists, *singles, stored)


def on_device(
    packed, block_dest, doc_len, w_qkv, b_qkv, w_out, b_out, norm1_gain, norm1_shift,
    w_glu, w_down, b_down, norm2_gain, norm2_shift, centroids, tile_list,
):
    seq_here = lax.axis_index("seq")
    batch_here = lax.axis_index("batch")

    def from_batch(values):
        far = {}
        for k in (1, 3, 2):
            turn = [(i, (i + k) % BATCHES) for i in range(BATCHES)]
            far[k] = lax.ppermute(values[k], "batch", turn)
        return [values[0], far[1], far[2], far[3]]

    received = lax.all_to_all(
        pack(packed, block_dest), "seq", split_axis=0, concat_axis=0, tiled=True
    )
    lists = jnp.concatenate(from_batch([tile_list] * BATCHES))
    info = jnp.stack([seq_here * SDEV, batch_here]).astype(jnp.int32)
    slopes = jnp.asarray(head_slopes(H) * np.float32(LOG2E))
    row = lambda v: v.reshape(1, -1)
    ws = (w_out, w_glu, w_down)
    vecs = (
        row(b_out), row(norm1_gain), row(norm1_shift),
        row(b_down), row(norm2_gain), row(norm2_shift), centroids,
    )
    x, q, kv, head, tail = project(
        pltpu.with_memory_space_constraint(received, pltpu.HBM), load(w_qkv), row(b_qkv)
    )
    up = [(i, i + 1) for i in range(NSEQ - 1)]
    down = [(j, i) for i, j in up]
    before = lax.ppermute(tail, "seq", up)
    after = lax.ppermute(head, "seq", down)
    scalars = (info, doc_len, lists, slopes)
    enc, tiles_12 = layer((1, 2), scalars, x, ws, x, q, kv, vecs)
    enc, *groups = layer(
        (0,), scalars, enc, ws, x, q, kv, vecs, halo=before, before=True, tiles_12=tiles_12
    )
    groups = from_batch(groups)
    enc, tile_3 = layer((3,), scalars, enc, ws, x, q, kv, vecs, halo=after, before=False)
    lasts = from_batch([tile_3] * BATCHES)
    stored = store_last(info, lists, lasts, store(info, groups))
    return enc, stored.reshape(1, 1, BATCHES * CAP * TROWS, D)


def solution(mesh):
    return jax.shard_map(
        on_device,
        mesh=mesh,
        in_specs=(
            P(("batch", "seq"), None),
            P(("batch", "seq")),
            P("batch"),
            P(), P(), P(), P(), P(), P(), P(), P(), P(), P(), P(), P(),
            P(("batch", "seq")),
        ),
        out_specs=(P(("batch", "seq"), None), P("batch", "seq", None, None)),
        check_vma=False,
    )
```

```python
import functools
import math

import jax
import jax.numpy as jnp
import numpy as np
from jax import lax
from jax.experimental import pallas as pl
from jax.experimental.pallas import tpu as pltpu
from jax.sharding import PartitionSpec as P

H = 12
D = 768
FF = 3072
DOC_LEN = 8192
BAND = 256
CAP = 2
TROWS = 128
LPO = 64
NSEQ = 32
BATCHES = 4
SDEV = 1024
BLK = 32
LEAD = 512
SPAN = NSEQ * SDEV
CH = 256
WIN = CH + 2 * BAND
HALF = CH // 2
KEYS = HALF + 2 * BAND
GROUPS = D // 128
PIECES = CAP * GROUPS * BLK
LABEL_ROWS = 16
LOADS = 4
FC = 768

norm_eps = 1e-06
LOG2E = math.log2(math.e)
FAR = -1e32
MIB = 1 << 20
KERNEL_VMEM = 20 * MIB
SMALL_VMEM = 8 * MIB
TINY_VMEM = MIB
PACK_VMEM = 56 * MIB
PROJECT_VMEM = 20 * MIB

ANY = pl.BlockSpec(memory_space=pl.ANY)
VMEM = pl.BlockSpec(memory_space=pltpu.VMEM)
SMEM = pl.BlockSpec(memory_space=pltpu.SMEM)
F32 = jnp.float32
BF16 = jnp.bfloat16


def head_slopes(heads):
    base = 2 ** int(np.floor(np.log2(heads)))
    first = [2.0 ** (-8.0 * (i + 1) / base) for i in range(base)]
    extra = [2.0 ** (-4.0 * (i + 1) / base) for i in range(2 * (heads - base))][0::2]
    return np.asarray(first + extra, np.float32)


def iota(shape, dim):
    return lax.broadcasted_iota(jnp.int32, shape, dim)


def dot(a, b):
    return jnp.dot(a, b, preferred_element_type=F32)


def piece(rank, group):
    return pl.ds(pl.multiple_of((rank * GROUPS + group) * BLK, BLK), BLK)


def pack_kernel(dest, packed_h, parts, packed, staged, labels, count, load_sems, sems, label_sem):
    step = SDEV // LOADS
    loads = [
        pltpu.make_async_copy(
            packed_h.at[pl.ds(i * step, step)], packed.at[pl.ds(i * step, step)], load_sems.at[i]
        )
        for i in range(LOADS)
    ]
    start_all(loads)
    labels[...] = jnp.zeros_like(labels)

    for i in range(NSEQ):
        count[i] = 0
    lane = iota((LABEL_ROWS, 128), 1)

    def copy_of(j, owner, rank):
        rows = pl.ds(pl.multiple_of(rank * GROUPS * BLK, GROUPS * BLK), GROUPS * BLK)
        return pltpu.make_async_copy(staged.at[j], parts.at[owner, rows], sems.at[j])

    def send(j, _):
        owner = lax.shift_right_logical(dest[j], 5)
        rank = count[owner]
        count[owner] = rank + 1
        rows = pl.ds(pl.multiple_of(j * BLK, BLK), BLK)
        for g in range(GROUPS):
            staged[j, g * BLK : (g + 1) * BLK] = packed[rows, g * 128 : (g + 1) * 128]
        copy_of(j, owner, rank).start()
        label = (dest[j] & (NSEQ - 1)) + 1
        new = jnp.where(lane == rank, label.astype(F32), labels[owner].astype(F32))
        labels[owner] = new.astype(BF16)
        return 0

    per = BLK // LOADS
    for i in range(LOADS):
        loads[i].wait()
        lax.fori_loop(i * per, (i + 1) * per, send, 0, unroll=True)
    last = pltpu.make_async_copy(labels, parts.at[:, pl.ds(PIECES, LABEL_ROWS)], label_sem)
    last.start()

    for j in range(BLK):
        copy_of(j, 0, 0).wait()
    last.wait()


def pack(packed, dest):
    return pl.pallas_call(
        pack_kernel,
        out_shape=jax.ShapeDtypeStruct((NSEQ, PIECES + LABEL_ROWS, 128), BF16),
        in_specs=[SMEM, ANY],
        out_specs=ANY,
        scratch_shapes=[
            pltpu.VMEM((SDEV, D), BF16),
            pltpu.VMEM((BLK, GROUPS * BLK, 128), BF16),
            pltpu.VMEM((NSEQ, LABEL_ROWS, 128), BF16),
            pltpu.SMEM((NSEQ,), jnp.int32),
            dma(LOADS),
            dma(BLK),
            dma(),
        ],
        compiler_params=pltpu.CompilerParams(vmem_limit_bytes=PACK_VMEM),
        name="pack_blocks",
    )(dest, packed)


def project_kernel(
    received_h, w_out_h, w_glu_h, w_down_h, w_qkv, b_qkv,
    x, q, kv, head, tail, w_out, w_glu, w_down,
    received, marks, vector, labels, where, sem, rsem, wsem,
):
    mark = pltpu.make_async_copy(received_h.at[:, pl.ds(PIECES, LABEL_ROWS)], marks, sem)
    mark.start()
    step = NSEQ // LOADS
    parts = [
        pltpu.make_async_copy(
            received_h.at[pl.ds(i * step, step), pl.ds(0, PIECES)],
            received.at[pl.ds(i * step, step)],
            rsem.at[i],
        )
        for i in range(LOADS)
    ]
    start_all(parts)
    weights = loads_of((w_out_h, w_glu_h, w_down_h), (w_out, w_glu, w_down), wsem)
    start_all(weights)
    mark.wait()
    vector[...] = jnp.max(marks[...].astype(F32), axis=1).astype(jnp.int32)
    copy = pltpu.make_async_copy(vector, labels, sem)
    copy.start()
    copy.wait()

    for source in range(NSEQ):
        for rank in range(CAP):
            where[labels[source, rank]] = source * CAP + rank
    wait_all(parts)

    def fetch(place, _):
        slot = where[1 + place]
        source = lax.shift_right_logical(slot, 1)
        rows = pl.ds(pl.multiple_of(place * BLK, BLK), BLK)
        for g in range(GROUPS):
            x[rows, g * 128 : (g + 1) * 128] = received[source, piece(slot & 1, g)]
        return 0

    lax.fori_loop(0, SDEV // BLK, fetch, 0, unroll=8)
    for i in range(2):
        columns = pl.ds((i + 1) * D, D)
        part = dot(x[...], w_qkv[:, columns]) + b_qkv[:, columns]
        kv[:, pl.ds(i * D, D)] = part.astype(BF16)
        head[:, pl.ds(i * D, D)] = part[:BAND].astype(BF16)
        tail[:, pl.ds(i * D, D)] = part[SDEV - BAND :].astype(BF16)
    q[...] = ((dot(x[...], w_qkv[:, :D]) + b_qkv[:, :D]) * (LOG2E / 8.0)).astype(BF16)
    wait_all(weights)


def project(received, ws, w_qkv, b_qkv):
    shapes = [(SDEV, D), (SDEV, D), (SDEV, 2 * D), (BAND, 2 * D), (BAND, 2 * D)]
    shapes += [w.shape for w in ws]
    return pl.pallas_call(
        project_kernel,
        out_shape=[jax.ShapeDtypeStruct(shape, BF16) for shape in shapes],
        in_specs=[ANY] * 4 + [VMEM] * 2,
        out_specs=[VMEM] * 8,
        scratch_shapes=[
            pltpu.VMEM((NSEQ, PIECES, 128), BF16),
            pltpu.VMEM((NSEQ, LABEL_ROWS, 128), BF16),
            pltpu.VMEM((NSEQ, 128), jnp.int32),
            pltpu.SMEM((NSEQ, 128), jnp.int32),
            pltpu.SMEM((SDEV // BLK + 1,), jnp.int32),
            dma(),
            dma(LOADS),
            dma(3),
        ],
        compiler_params=pltpu.CompilerParams(vmem_limit_bytes=PROJECT_VMEM),
        name="project_tokens",
    )(received, *ws, w_qkv, b_qkv)


def load_kernel(source, target, sem):
    copy = pltpu.make_async_copy(source, target, sem)
    copy.start()
    copy.wait()


def load(w):
    return pl.pallas_call(
        load_kernel,
        out_shape=jax.ShapeDtypeStruct(w.shape, w.dtype),
        in_specs=[ANY],
        out_specs=VMEM,
        scratch_shapes=[dma()],
        compiler_params=pltpu.CompilerParams(vmem_limit_bytes=TINY_VMEM),
        cost_estimate=pl.CostEstimate(flops=0, bytes_accessed=2 * w.size, transcendentals=0),
        name="load_weights",
    )(w)


def doc_bounds(info, doc_len, start):
    u0 = info[0] + LEAD + start
    doc = lax.shift_right_logical(u0, 13)
    base = doc * DOC_LEN
    length = doc_len[doc]
    low = jnp.maximum(0, LEAD - base)
    high = jnp.minimum(length, SPAN + LEAD - base)
    return u0 - base, length, low, high


def reach_table(info, doc_len, start):
    rel, _, low, high = doc_bounds(info, doc_len, start)
    j = iota((CH, WIN), 1)
    dist = jnp.abs(iota((CH, WIN), 0) + BAND - j)
    key = rel - BAND + j
    keep = (dist <= BAND) & (((key >= low) & (key < high)) | (dist == 0))
    return jnp.where(keep, -dist.astype(F32), FAR)


def layer_norm(v, gain, shift):
    centre = jnp.mean(v, axis=-1, keepdims=True)
    v = v - centre
    spread = jnp.mean(v * v, axis=-1, keepdims=True)
    return v * lax.rsqrt(spread + norm_eps) * gain + shift


def gelu(x):
    z = jnp.abs(x)
    t = 1.0 / (1.0 + z * (0.3275911 * math.sqrt(0.5)))
    p = t * (0.5 * 1.061405429) + (0.5 * -1.453152027)
    p = p * t + (0.5 * 1.421413741)
    p = p * t + (0.5 * -0.284496736)
    p = p * t + (0.5 * 0.254829592)
    q = p * t * jnp.exp2(x * x * (-0.5 * LOG2E))
    return jnp.maximum(x, 0.0) - z * q


def attend_pair(pair, chunks, q, window, reach, slopes, att):
    lanes = pl.ds(pair * 128, 128)
    vlanes = pl.ds(D + pair * 128, 128)
    left = iota((CH, 128), 1) < 64
    ones = jnp.ones((WIN, 128), BF16)
    outside = jnp.zeros((HALF, WIN - KEYS), BF16)
    for n, c in enumerate(chunks):
        mine = q[pl.ds(c * CH, CH), lanes]
        none = jnp.zeros_like(mine)
        both = jnp.concatenate([jnp.where(left, mine, none), jnp.where(left, none, mine)], axis=0)
        scores = lax.dot_general(
            both, window(c, lanes), (((1,), (1,)), ((), ())), preferred_element_type=F32
        )
        probs = []
        for side in range(2):
            for half in range(2):
                row = half * HALF
                keys = slice(half * HALF, half * HALF + KEYS)
                s = scores[side * CH + row : side * CH + row + HALF, keys]
                s = s + slopes[2 * pair + side] * reach[n, row : row + HALF, keys]
                p = jnp.exp2(s - jnp.max(s, axis=-1, keepdims=True)).astype(BF16)
                probs.append(jnp.concatenate([outside, p] if half else [p, outside], axis=1))
        v = jnp.concatenate([window(c, vlanes), ones], axis=1)
        o = dot(jnp.concatenate(probs, axis=0), v)
        o = o[:, :128] / o[:, 128:]
        att[pl.ds(n * CH, CH), lanes] = jnp.where(left, o[:CH], o[CH:]).astype(BF16)


def pool_tile(info, doc_len, lists, chunk, enc, centroids):
    rel, length, _, _ = doc_bounds(info, doc_len, chunk * CH)
    r = iota((TROWS, CH), 0)
    i = iota((TROWS, CH), 1)
    scale = jnp.where(length - rel - 2 * r >= 2, 0.5, 1.0)
    mine = (lax.shift_right_logical(i, 1) == r) & (rel + i < length)
    pooled = dot(jnp.where(mine, scale, 0.0).astype(BF16), enc)
    pick = (iota((TROWS, centroids.shape[0]), 1) == lists[chunk]).astype(BF16)
    return (pooled - dot(pick, centroids[...])).astype(BF16)


def start_all(copies):
    for c in copies:
        c.start()


def wait_all(copies):
    for c in copies:
        c.wait()


def layer_of(att, x, start, first, active, enc, ws, vecs):
    w_out, w_glu, w_down = ws
    b_out, g1, s1, b_down, g2, s2 = vecs
    count = att.shape[0]
    part = count // 2
    for r in range(0, count, part):
        rows = pl.ds(r, part)
        mixed = dot(att[rows], w_out[...]) + b_out[...] + x[pl.ds(start + r, part)].astype(F32)
        first[rows] = layer_norm(mixed, g1[...], s1[...]).astype(BF16)
    for i in range(FF // FC):
        cols = pl.ds(i * FC, FC)
        up = pl.ds(FF + i * FC, FC)
        f = first[...]
        active[:, cols] = (gelu(dot(f, w_glu[:, cols])) * dot(f, w_glu[:, up])).astype(BF16)
    for r in range(0, count, part):
        rows = pl.ds(r, part)
        second = dot(active[rows], w_down[...]) + b_down[...] + first[rows].astype(F32)
        enc[rows] = layer_norm(second, g2[...], s2[...]).astype(BF16)


def loads_of(sources, targets, sems):
    return [pltpu.make_async_copy(s, t, sems.at[i]) for i, (s, t) in enumerate(zip(sources, targets))]


def layer_kernel(
    chunks, before, info, doc_len, lists, slopes,
    enc_in, w_out, w_glu, w_down, x, q, kv, *rest,
):
    halo = None if before is None else rest[0]
    b_out, g1, s1, b_down, g2, s2, centroids = rest[:7] if halo is None else rest[1:8]
    enc_h, *tiles, att, first, active, reach, enc, osem = rest[
        {None: 7, True: 9, False: 8}[before] :
    ]
    ws = (w_out, w_glu, w_down)
    start = chunks[0] * CH
    rows = len(chunks) * CH
    for n, c in enumerate(chunks):
        reach[n] = reach_table(info, doc_len, c * CH)

    def window(c, lanes):
        if halo is None:
            return kv[pl.ds(c * CH - BAND, WIN), lanes]
        own = kv[pl.ds(0 if before else c * CH - BAND, WIN - BAND), lanes]
        return jnp.concatenate([halo[:, lanes], own] if before else [own, halo[:, lanes]], axis=0)

    for pair in range(H // 2):
        attend_pair(pair, chunks, q, window, reach, slopes, att)
    layer_of(att, x, start, first, active, enc, ws, (b_out, g1, s1, b_down, g2, s2))
    last = pltpu.make_async_copy(enc, enc_h.at[pl.ds(start, rows)], osem)
    last.start()
    for n, c in enumerate(chunks):
        tile = pool_tile(info, doc_len, lists, c, enc[pl.ds(n * CH, CH)], centroids)
        if before:
            att[pl.ds(0, TROWS)] = tile
            send_tiles(info, lists, att.at[pl.ds(0, TROWS)], rest[8], tiles)
        else:
            tiles[0][n] = tile
    last.wait()


def send_tiles(info, lists, tile_0, tiles_12, groups):
    owners = [lax.shift_right_logical(lists[t], 6) for t in range(3)]
    for g in groups:
        g[...] = jnp.zeros_like(g)
    for t in range(3):
        rank = sum([(owners[e] == owners[t]).astype(jnp.int32) for e in range(t)], jnp.int32(0))
        turn = (owners[t] + BATCHES - info[1]) & (BATCHES - 1)
        for k, g in enumerate(groups):

            @pl.when(turn == k)
            def _():
                g[rank] = tile_0[...] if t == 0 else tiles_12[t - 1]


def dma(*shape):
    return pltpu.SemaphoreType.DMA(shape)


def layer(chunks, scalars, enc, ws, x, q, kv, vecs, halo=None, before=None, tiles_12=None):
    rows = len(chunks) * CH
    rest = (x, q, kv) + (() if halo is None else (halo,)) + vecs
    rest += () if tiles_12 is None else (tiles_12,)
    tiles = [(CAP, TROWS, D)] * BATCHES if before else [(len(chunks), TROWS, D)]
    return pl.pallas_call(
        functools.partial(layer_kernel, chunks, before),
        out_shape=(
            jax.ShapeDtypeStruct((SDEV, D), BF16),
            *[jax.ShapeDtypeStruct(shape, BF16) for shape in tiles],
        ),
        in_specs=[SMEM] * 4 + [ANY] + [VMEM] * (3 + len(rest)),
        out_specs=(ANY,) + (VMEM,) * len(tiles),
        input_output_aliases={} if halo is None else {4: 0},
        scratch_shapes=[
            pltpu.VMEM((rows, D), BF16),
            pltpu.VMEM((rows, D), BF16),
            pltpu.VMEM((rows, FF), BF16),
            pltpu.VMEM((len(chunks), CH, WIN), F32),
            pltpu.VMEM((rows, D), BF16),
            dma(),
        ],
        compiler_params=pltpu.CompilerParams(vmem_limit_bytes=KERNEL_VMEM),
        cost_estimate=pl.CostEstimate(
            flops=12_000_000 * rows, bytes_accessed=20_000_000, transcendentals=16_000 * rows
        ),
        name="layer_chunk_%d" % chunks[0],
    )(*scalars, enc, *ws, *rest)


def store_kernel(info, *refs):
    groups, out, sems = refs[:BATCHES], refs[BATCHES], refs[BATCHES + 1]
    moves = []
    for k in range(BATCHES):
        device = (info[1] + BATCHES - k) & (BATCHES - 1)
        for r in range(CAP):
            row = pl.multiple_of((device * CAP + r) * TROWS, TROWS)
            dst = out.at[pl.ds(row, TROWS)]
            moves.append(pltpu.make_async_copy(groups[k].at[r], dst, sems.at[k * CAP + r]))
    start_all(moves)
    wait_all(moves)


def store(info, groups):
    return pl.pallas_call(
        store_kernel,
        out_shape=jax.ShapeDtypeStruct((BATCHES * CAP * TROWS, D), BF16),
        in_specs=[SMEM] + [VMEM] * BATCHES,
        out_specs=ANY,
        scratch_shapes=[dma(BATCHES * CAP)],
        compiler_params=pltpu.CompilerParams(vmem_limit_bytes=SMALL_VMEM),
        name="store_tiles",
    )(info, *groups)


def store_last_kernel(info, lists, *refs):
    singles, out, sems = refs[:BATCHES], refs[BATCHES + 1], refs[BATCHES + 2]
    moves = []
    for k in range(BATCHES):
        device = (info[1] + BATCHES - k) & (BATCHES - 1)
        mine = [lax.shift_right_logical(lists[k * 4 + t], 6) == info[1] for t in range(4)]
        rank = sum([m.astype(jnp.int32) for m in mine[:3]], jnp.int32(0))
        row = pl.multiple_of((device * CAP + jnp.minimum(rank, CAP - 1)) * TROWS, TROWS)
        dst = out.at[pl.ds(row, TROWS)]
        moves.append((mine[3], pltpu.make_async_copy(singles[k].at[0], dst, sems.at[k])))
    for go, copy in moves:
        pl.when(go)(copy.start)
    for go, copy in moves:
        pl.when(go)(copy.wait)


def store_last(info, lists, singles, stored):
    return pl.pallas_call(
        store_last_kernel,
        out_shape=jax.ShapeDtypeStruct(stored.shape, BF16),
        in_specs=[SMEM] * 2 + [VMEM] * BATCHES + [ANY],
        out_specs=ANY,
        input_output_aliases={2 + BATCHES: 0},
        scratch_shapes=[dma(BATCHES)],
        compiler_params=pltpu.CompilerParams(vmem_limit_bytes=SMALL_VMEM),
        name="store_last_tile",
    )(info, lists, *singles, stored)


def on_device(
    packed, block_dest, doc_len, w_qkv, b_qkv, w_out, b_out, norm1_gain, norm1_shift,
    w_glu, w_down, b_down, norm2_gain, norm2_shift, centroids, tile_list,
):
    seq_here = lax.axis_index("seq")
    batch_here = lax.axis_index("batch")

    def from_batch(values):
        far = {}
        for k in (1, 3, 2):
            turn = [(i, (i + k) % BATCHES) for i in range(BATCHES)]
            far[k] = lax.ppermute(values[k], "batch", turn)
        return [values[0], far[1], far[2], far[3]]

    received = lax.all_to_all(
        pack(packed, block_dest), "seq", split_axis=0, concat_axis=0, tiled=True
    )
    lists = jnp.concatenate(from_batch([tile_list] * BATCHES))
    info = jnp.stack([seq_here * SDEV, batch_here]).astype(jnp.int32)
    slopes = jnp.asarray(head_slopes(H) * np.float32(LOG2E))
    row = lambda v: v.reshape(1, -1)
    vecs = (
        row(b_out), row(norm1_gain), row(norm1_shift),
        row(b_down), row(norm2_gain), row(norm2_shift), centroids,
    )
    far = lambda v: pltpu.with_memory_space_constraint(v, pltpu.HBM)
    ws = tuple(far(w) for w in (w_out, w_glu, w_down))
    x, q, kv, head, tail, *ws = project(far(received), ws, load(w_qkv), row(b_qkv))
    up = [(i, i + 1) for i in range(NSEQ - 1)]
    down = [(j, i) for i, j in up]
    before = lax.ppermute(tail, "seq", up)
    after = lax.ppermute(head, "seq", down)
    scalars = (info, doc_len, lists, slopes)
    enc, tiles_12 = layer((1, 2), scalars, x, ws, x, q, kv, vecs)
    enc, *groups = layer(
        (0,), scalars, enc, ws, x, q, kv, vecs, halo=before, before=True, tiles_12=tiles_12
    )
    groups = from_batch(groups)
    enc, tile_3 = layer((3,), scalars, enc, ws, x, q, kv, vecs, halo=after, before=False)
    lasts = from_batch([tile_3] * BATCHES)
    stored = store_last(info, lists, lasts, store(info, groups))
    return enc, stored.reshape(1, 1, BATCHES * CAP * TROWS, D)


def solution(mesh):
    return jax.shard_map(
        on_device,
        mesh=mesh,
        in_specs=(
            P(("batch", "seq"), None),
            P(("batch", "seq")),
            P("batch"),
            P(), P(), P(), P(), P(), P(), P(), P(), P(), P(), P(), P(),
            P(("batch", "seq")),
        ),
        out_specs=(P(("batch", "seq"), None), P("batch", "seq", None, None)),
        check_vma=False,
    )
```
